512 devices in a mesh: dp: 8 (over x, y_hi), seq: 64 (over z, y_lo, core).
Axes of the slice: x: 4, y: 4 (y_hi: 2, y_lo: 2; y = y_hi * 2 + y_lo), z: 16, core: 2. Of those that a mesh axis runs over, the one named last changes fastest.
Arguments:
- tokens: bfloat16 [8, 64, 256, 1024], P('dp', 'seq'), may hold values from -24 to 24
- cotangent: bfloat16 [8, 64, 256, 1024], P('dp', 'seq'), may hold values from -16 to 16
- row_mask: int32 [4, 64, 2, 2], P(None, 'seq'), may hold values from 0 to 1, as said below
- column_mask: int32 [4, 256, 8, 8], P(None, 'seq'), may hold values from 0 to 1, as said below
- w_query: bfloat16 [1024, 512], P('dp'), may hold values from -0.25 to 0.25
- w_key: bfloat16 [1024, 512], P('dp'), may hold values from -0.25 to 0.25
- w_value: bfloat16 [1024, 512], P('dp'), may hold values from -0.1875 to 0.1875
- w_out: bfloat16 [512, 1024], P('dp'), may hold values from -0.25 to 0.25
Outputs:
- mixed: bfloat16 [8, 64, 256, 1024], P('dp', 'seq')
- grad_tokens: bfloat16 [8, 64, 256, 1024], P('dp', 'seq')
- grad_value: float32 [1024, 512], P(('dp', 'seq'))
- grad_output: float32 [512, 1024], P(None, ('dp', 'seq'))
The draws below stay inside these ranges and needn't reach their ends.
Inputs may be any that keep to these rules, and one draw needn't show every extreme that they name: `row_mask`: each block mask is lower triangular with ones on its diagonal. `column_mask`: each block mask is lower triangular with ones on its diagonal.
All inputs are finite; a program needn't handle non-finite values.
Results may differ from the reference program's by a relative error of at most 0.015.
Values may be sent and summed in bfloat16 or wider, within the bound.
No kernel may reach another device: no remote copies, remote signals or barrier semaphores. Data moves between devices by JAX's collectives and lax.ppermute only.
A program may use at most 64 MiB of HBM per device.

```python
import math
import jax
import jax.numpy as jnp
from jax import lax

D = 1024
HEADS = 8
HEAD_DIM = 64
GC = 256
ROWBLK = 128
COLBLK = 8
HALF_HEADS = 4
HD = 512
GR = 64
SEQS = 8
NBR = 2
NBC = 8


def shared_projection(key):
    return jax.random.normal(key, (D, HD))


def draw_w_query(key, part):
    common = shared_projection(key)
    return jnp.clip(common * D ** (-0.5), -0.25, 0.25).astype(jnp.bfloat16)


def draw_w_key(key, part):
    key = jax.random.fold_in(key, 22)
    own_part = jax.random.normal(key, (D, HD))
    mixture = own_part
    return jnp.clip(mixture * D ** (-0.5), -0.25, 0.25).astype(jnp.bfloat16)


def random_blocks(key, heads, lines, blocks):
    bits = jax.random.randint(key, (heads, lines, blocks, blocks), 0, 2)
    lower = jnp.arange(blocks)[:, None] > jnp.arange(blocks)[None, :]
    diagonal = jnp.arange(blocks)[:, None] == jnp.arange(blocks)[None, :]
    return jnp.where(lower, bits, 0) + diagonal.astype(jnp.int32)


def draw_row_mask(key, part):
    key = jax.random.fold_in(key, 31)
    return random_blocks(key, HALF_HEADS, GR, NBR).astype(jnp.int32)


def draw_column_mask(key, part):
    key = jax.random.fold_in(key, 32)
    return random_blocks(key, HALF_HEADS, GC, NBC).astype(jnp.int32)


def draw_tokens(key, part):
    key = jax.random.fold_in(key, 11)
    keys = jax.random.split(key, 1)
    shape = (SEQS, GR, GC, D)
    base = jax.random.normal(keys[0], shape)
    return jnp.clip(base, -6.0, 6.0).astype(jnp.bfloat16)


def with_spikes(values, rng, source, target, blocks, factor):
    def block_of(position):
        return (jnp.arange(values.shape[position]) // (values.shape[position] // blocks)).reshape((-1,) + (1,) * (values.ndim - 1 - position))

    near = jax.random.permutation(rng, blocks)[block_of(target)]
    other_side = (block_of(target) + blocks // 2) % blocks
    return jnp.where((block_of(source) == near) | (block_of(source) == other_side), factor * values, values)


def levels(stream_key, shape, shards, least, largest):
    gain = 1.0
    for dim, blocks in shards:
        steps = jax.random.uniform(jax.random.fold_in(jax.random.fold_in(stream_key, 6), dim), (blocks,), jnp.float32, least / len(shards), largest / len(shards))
        gain = gain * jnp.repeat(jnp.exp(steps), shape[dim] // blocks).reshape((-1,) + (1,) * (len(shape) - 1 - dim))
    return gain


def bell_draw(stream_key, dims, deviation, most, shards=(), held_as=jnp.bfloat16):
    drawn = jax.random.normal(stream_key, dims, jnp.float32) * deviation
    if len(shards) > 0:
        drawn = levels(stream_key, dims, shards, -0.22, 0.18) * drawn
    return jnp.clip(drawn, min=-most, max=most).astype(held_as)


def bell_draw_with(stream_key, extent, deviation, reach, cuts, heavy, kind=jnp.bfloat16):
    values = deviation * jax.random.normal(stream_key, extent, jnp.float32)
    if cuts:
        values = values * levels(stream_key, extent, cuts, -0.22, 0.18)
    return jnp.clip(with_spikes(values, jax.random.fold_in(stream_key, 3), *heavy), -reach, reach).astype(kind)


def setup_inputs(seed: int = 0) -> dict:
    arg_keys = jax.random.split(jax.random.key(seed), 9)
    return {
        "tokens": draw_tokens(jax.random.fold_in(arg_keys[8], 71), 0),
        "cotangent": bell_draw_with(arg_keys[1], (SEQS, GR, GC, D), 1.0, 16.0, ((0, 8), (1, 64)), (1, 3, 64, 4.0)),
        "row_mask": draw_row_mask(jax.random.fold_in(arg_keys[8], 71), 0),
        "column_mask": draw_column_mask(jax.random.fold_in(arg_keys[8], 71), 0),
        "w_query": draw_w_query(jax.random.fold_in(arg_keys[8], 71), 0),
        "w_key": draw_w_key(jax.random.fold_in(arg_keys[8], 71), 0),
        "w_value": bell_draw(arg_keys[6], (D, HD), D ** -0.5, 0.1875, ((0, 8),)),
        "w_out": bell_draw(arg_keys[7], (HD, D), HD ** -0.5, 0.25, ((0, 8),)),
    }


row_forms = ('blhe,bmhe->bhlm', 'bhlm,bmhe->blhe')
column_forms = ('lbhe,mbhe->bhlm', 'bhlm,mbhe->lbhe')
contract_last = (((1,), (1,)), ((), ()))
contract_first = (((0,), (0,)), ((), ()))

def allowed_cells(mask_blocks, block_size):
    expanded = jnp.repeat(jnp.repeat(mask_blocks, block_size, axis=-2), block_size, axis=-1)
    length = expanded.shape[-1]
    causal = jnp.arange(length)[:, None] >= jnp.arange(length)[None, :]
    return (expanded == 1) & causal

def attend(queries, key_part, value_part, allowed, forms):
    scale_factor = 1.0 / math.sqrt(queries.shape[-1])
    scores = jnp.einsum(forms[0], queries.astype(jnp.float32), key_part.astype(jnp.float32)) * scale_factor
    scores = jnp.where(allowed, scores, -1e+30)
    highest = lax.stop_gradient(lax.optimization_barrier(jnp.max(scores, axis=-1, keepdims=True)))
    weights = jnp.exp(scores - highest)
    weights = weights / lax.optimization_barrier(jnp.sum(weights, axis=-1, keepdims=True))
    rounded = lax.optimization_barrier(weights.astype(jnp.bfloat16)).astype(jnp.float32)
    result = jnp.einsum(forms[1], rounded, value_part.astype(jnp.float32))
    return result.astype(jnp.bfloat16)

def layer(sequence, cot_seq, row_mask, column_mask, w_query, w_key, w_value, w_out):
    grid_rows, grid_cols, width = sequence.shape
    flat = sequence.reshape(-1, width)
    cot_flat = cot_seq.reshape(-1, width)
    half = HEADS // 2

    def project(weight):
        product = jnp.dot(flat, weight, preferred_element_type=jnp.float32).astype(jnp.bfloat16)
        return product.reshape(grid_rows, grid_cols, HEADS, HEAD_DIM)
    row_allowed = allowed_cells(jnp.transpose(row_mask, (1, 0, 2, 3)), ROWBLK)
    column_allowed = allowed_cells(jnp.transpose(column_mask, (1, 0, 2, 3)), COLBLK)

    def core(query_all, key_all, value_all):
        row_out = attend(query_all[:, :, :half], key_all[:, :, :half], value_all[:, :, :half], row_allowed, row_forms)
        column_out = attend(query_all[:, :, half:], key_all[:, :, half:], value_all[:, :, half:], column_allowed, column_forms)
        return jnp.concatenate([row_out, column_out], axis=2)
    heads_out, core_back = jax.vjp(core, project(w_query), project(w_key), project(w_value))
    attended = heads_out.reshape(-1, HD)
    mixed = jnp.dot(attended, w_out, preferred_element_type=jnp.float32).astype(jnp.bfloat16)
    grad_heads = lax.dot_general(cot_flat, w_out, contract_last, preferred_element_type=jnp.float32).astype(jnp.bfloat16)
    grads = core_back(grad_heads.reshape(grid_rows, grid_cols, HEADS, HEAD_DIM))

    def back(grad, weight):
        return lax.dot_general(grad.reshape(-1, HD), weight, contract_last, preferred_element_type=jnp.float32)
    grad_tokens = (back(grads[0], w_query) + back(grads[1], w_key) + back(grads[2], w_value)).astype(jnp.bfloat16)
    value_term = lax.dot_general(flat, grads[2].reshape(-1, HD), contract_first, preferred_element_type=jnp.float32)
    out_term = lax.dot_general(attended, cot_flat, contract_first, preferred_element_type=jnp.float32)
    return (mixed.reshape(sequence.shape), grad_tokens.reshape(sequence.shape), value_term, out_term)

def reference(tokens, cotangent, row_mask, column_mask, w_query, w_key, w_value, w_out):

    def step(carry, pair):
        mixed, grad_tokens, value_term, out_term = layer(pair[0], pair[1], row_mask, column_mask, w_query, w_key, w_value, w_out)
        return ((carry[0] + value_term, carry[1] + out_term), (mixed, grad_tokens))
    start = (jnp.zeros((D, HD), jnp.float32), jnp.zeros((HD, D), jnp.float32))
    totals, stacked = lax.scan(step, start, (tokens, cotangent))
    return (stacked[0], stacked[1], totals[0], totals[1])
```

```python
import functools

import jax
import jax.numpy as jnp
from jax import lax
from jax.experimental import pallas as pl
from jax.experimental.pallas import tpu as pltpu
from jax.sharding import Mesh, PartitionSpec as P

HEAD_DIM = 64
ROWBLK = 128
COLBLK = 8
BF = jnp.bfloat16
F32 = jnp.float32
LAST = (((1,), (1,)), ((), ()))
FIRST = (((0,), (0,)), ((), ()))
MASKED = -1e30


def weight_copies(core, own, other, slots, wo_ref, sems, kinds):
    copies = []
    for k, kind in enumerate(kinds):
        for half, src in ((core, own), (1 - core, other)):
            for b in range(2):
                copies.append(
                    pltpu.make_async_copy(
                        src.at[pl.ds(kind * 4, 4), pl.ds(b * 64, 64), pl.ds(768, 256)],
                        wo_ref.at[k, half * 2 + b],
                        sems.at[len(copies)],
                    )
                )
    return copies


def head_kernel(
    kind,
    core_ref,
    x_ref,
    ct_ref,
    bias_ref,
    own_ref,
    other_ref,
    parts_ref,
    keep_ref,
    send_ref,
    wqkv,
    wo,
    sems,
):
    core = core_ref[0]
    copies = weight_copies(core, own_ref, other_ref, None, wo, sems, (kind,))
    projections = pl.ds(0, 768)

    @pl.when(core == kind)
    def _():
        pltpu.make_async_copy(own_ref.at[:, :, projections], wqkv, sems.at[4]).start()

    @pl.when(core != kind)
    def _():
        pltpu.make_async_copy(other_ref.at[:, :, projections], wqkv, sems.at[4]).start()

    for copy in copies:
        copy.start()
    pltpu.make_async_copy(own_ref.at[:, :, projections], wqkv, sems.at[4]).wait()
    for copy in copies:
        copy.wait()

    x = x_ref[...]
    ct = ct_ref[...]
    width = x.shape[1]
    qkv = jnp.dot(x, wqkv[...].reshape(width, 768), preferred_element_type=F32).astype(BF)
    q, k, v = qkv[:, :256], qkv[:, 256:512], qkv[:, 512:]
    do = jnp.zeros((x.shape[0], 256), F32)
    for block in range(4):
        do += lax.dot_general(
            ct[:, block * 256 : (block + 1) * 256],
            wo[0, block].reshape(256, 256),
            LAST,
            preferred_element_type=F32,
        )
    do = do.astype(BF)
    lane = lax.broadcasted_iota(jnp.int32, (x.shape[0], 256), 1) // HEAD_DIM
    zero = jnp.zeros_like(q)
    out = jnp.zeros((x.shape[0], 256), F32)
    dq, dk, dv = out, out, out
    for h in range(4):
        mine = lane == h
        kh, vh = jnp.where(mine, k, zero), jnp.where(mine, v, zero)
        qh, doh = jnp.where(mine, q, zero), jnp.where(mine, do, zero)
        s = lax.dot_general(q, kh, LAST, preferred_element_type=F32) * 0.125
        s = s + bias_ref[h].astype(F32)
        e = jnp.exp(s - jnp.max(s, axis=-1, keepdims=True))
        w = e * (1.0 / jnp.sum(e, axis=-1, keepdims=True))
        p = w.astype(BF)
        out += jnp.dot(p, vh, preferred_element_type=F32)
        dp = lax.dot_general(do, vh, LAST, preferred_element_type=F32).astype(BF).astype(F32)
        ds = w * (dp - jnp.sum(dp * w, axis=-1, keepdims=True)) * 0.125
        ds = ds.astype(BF)
        dq += jnp.dot(ds, kh, preferred_element_type=F32)
        dk += lax.dot_general(ds, qh, FIRST, preferred_element_type=F32)
        dv += lax.dot_general(p, doh, FIRST, preferred_element_type=F32)
    out, dv = out.astype(BF), dv.astype(BF)
    parts_ref[:, 0:256] = out
    parts_ref[:, 256:512] = dq.astype(BF)
    parts_ref[:, 512:768] = dk.astype(BF)
    parts_ref[:, 768:1024] = dv
    grad_value = lax.dot_general(x, dv, FIRST, preferred_element_type=F32).astype(BF)
    grad_out = lax.dot_general(ct, out, FIRST, preferred_element_type=F32).astype(BF)

    @pl.when(core == 0)
    def _():
        keep_ref[...] = grad_value
        send_ref[...] = grad_out

    @pl.when(core != 0)
    def _():
        keep_ref[...] = grad_out
        send_ref[...] = grad_value


def heads_call(kind, core, x, ct, bias, own, other):
    rows, width = x.shape
    vmem = pl.BlockSpec(memory_space=pltpu.VMEM)
    return pl.pallas_call(
        functools.partial(head_kernel, kind),
        out_shape=(
            jax.ShapeDtypeStruct((rows, 1024), BF),
            jax.ShapeDtypeStruct((width, 256), BF),
            jax.ShapeDtypeStruct((width, 256), BF),
        ),
        in_specs=[
            pl.BlockSpec(memory_space=pltpu.SMEM),
            vmem,
            vmem,
            vmem,
            pl.BlockSpec(memory_space=pl.ANY),
            pl.BlockSpec(memory_space=pl.ANY),
        ],
        out_specs=(vmem, vmem, vmem),
        scratch_shapes=[
            pltpu.VMEM((8, 128, 768), BF),
            pltpu.VMEM((1, 4, 4, 64, 256), BF),
            pltpu.SemaphoreType.DMA((5,)),
        ],
        compiler_params=pltpu.CompilerParams(vmem_limit_bytes=40 * 1024 * 1024),
        cost_estimate=pl.CostEstimate(flops=1400000000, bytes_accessed=6000000, transcendentals=262144),
        name="row_heads" if kind == 0 else "column_heads",
    )(core, x, ct, bias, own, other)


def final_kernel(core_ref, row_ref, col_ref, own_ref, other_ref, mixed_ref, gt_ref, wqkv, wo, sems):
    core = core_ref[0]
    copies = weight_copies(core, own_ref, other_ref, None, wo, sems, (0, 1))
    for half, src in ((core, own_ref), (1 - core, other_ref)):
        copies.append(
            pltpu.make_async_copy(src.at[:, :, pl.ds(0, 768)], wqkv.at[half], sems.at[len(copies)])
        )
    for copy in copies:
        copy.start()
    for copy in copies:
        copy.wait()
    sides = (row_ref[...], col_ref[...])
    for block in range(4):
        total = jnp.zeros((row_ref.shape[0], 256), F32)
        for kind in range(2):
            total += jnp.dot(
                sides[kind][:, :256], wo[kind, block].reshape(256, 256), preferred_element_type=F32
            )
        mixed_ref[:, block * 256 : (block + 1) * 256] = total.astype(BF)
    total = jnp.zeros(gt_ref.shape, F32)
    for kind in range(2):
        total += lax.dot_general(
            sides[kind][:, 256:],
            wqkv[kind].reshape(1024, 768),
            LAST,
            preferred_element_type=F32,
        )
    gt_ref[...] = total.astype(BF)


def final_call(core, row_parts, col_parts, own, other):
    rows = row_parts.shape[0]
    vmem = pl.BlockSpec(memory_space=pltpu.VMEM)
    anywhere = pl.BlockSpec(memory_space=pl.ANY)
    return pl.pallas_call(
        final_kernel,
        out_shape=(
            jax.ShapeDtypeStruct((rows, 1024), BF),
            jax.ShapeDtypeStruct((rows, 1024), BF),
        ),
        in_specs=[pl.BlockSpec(memory_space=pltpu.SMEM), vmem, vmem, anywhere, anywhere],
        out_specs=(vmem, vmem),
        scratch_shapes=[
            pltpu.VMEM((2, 8, 128, 768), BF),
            pltpu.VMEM((2, 4, 4, 64, 256), BF),
            pltpu.SemaphoreType.DMA((10,)),
        ],
        compiler_params=pltpu.CompilerParams(vmem_limit_bytes=40 * 1024 * 1024),
        cost_estimate=pl.CostEstimate(flops=1100000000, bytes_accessed=6000000, transcendentals=0),
        name="output_products",
    )(core, row_parts, col_parts, own, other)


def one_hot(index, size):
    return (index[:, None] == jnp.arange(size)[None, :]).astype(BF)


def biases(row_mask, column_mask):
    position = jnp.arange(256)
    seen = position[:, None] >= position[None, :]
    row_in = one_hot(position // ROWBLK, 2)
    row_blocks = jnp.einsum(
        "ia,hab,jb->hij", row_in, row_mask[:, 0].astype(BF), row_in, preferred_element_type=BF
    )
    same = (position[:, None] % 4) == (position[None, :] % 4)
    col_left = one_hot((position % 4) * 8 + position // (4 * COLBLK), 32)
    col_right = one_hot(position // (4 * COLBLK), 8)
    col_blocks = jnp.einsum(
        "ia,hab,jb->hij",
        col_left,
        column_mask.reshape(4, 32, 8).astype(BF),
        col_right,
        preferred_element_type=BF,
    )
    row_bias = jnp.where((row_blocks > 0.5) & seen, 0.0, MASKED).astype(BF)
    col_bias = jnp.where((col_blocks > 0.5) & seen & same, 0.0, MASKED).astype(BF)
    return row_bias, col_bias


def body(tokens, cotangent, row_mask, column_mask, w_query, w_key, w_value, w_out):
    core = lax.axis_index("c")
    core_arg = core.astype(jnp.int32).reshape(1)
    flat = tokens.reshape(256, 1024)
    cot_flat = cotangent.reshape(256, 1024)
    seq = ("z", "yl", "c")

    def to_columns(matrix):
        moved = lax.all_to_all(
            matrix.reshape(64, 4, 1024), seq, split_axis=0, concat_axis=0, tiled=True
        )
        return moved.reshape(256, 1024)

    with jax.named_scope("weights"):
        def half_of(weight):
            return lax.dynamic_slice_in_dim(weight, core * 256, 256, axis=1)

        out_half = lax.dynamic_slice_in_dim(w_out, core * 512, 512, axis=1)
        packed = jnp.concatenate(
            [
                half_of(w_query),
                half_of(w_key),
                half_of(w_value),
                jnp.concatenate([out_half[:, :256], out_half[:, 256:]], axis=0),
            ],
            axis=1,
        )
        own = lax.all_to_all(
            jnp.broadcast_to(packed[None], (8, 128, 1024)),
            ("x", "yh"),
            split_axis=0,
            concat_axis=0,
            tiled=True,
        )
        other = lax.ppermute(own, "c", [(0, 1), (1, 0)])
    with jax.named_scope("to_columns"):
        col_tokens = to_columns(flat)
        col_cot = to_columns(cot_flat)
    with jax.named_scope("masks"):
        row_bias, col_bias = biases(row_mask, column_mask)
    row_parts, row_keep, row_send = heads_call(0, core_arg, flat, cot_flat, row_bias, own, other)
    col_parts, col_keep, col_send = heads_call(
        1, core_arg, col_tokens, col_cot, col_bias, own, other
    )
    with jax.named_scope("from_columns"):
        returned = lax.all_to_all(
            col_parts.reshape(64, 4, 1024), seq, split_axis=0, concat_axis=0, tiled=True
        ).reshape(256, 1024)
    with jax.named_scope("gradient_sums"):
        def core_sum(keep, send):
            got = lax.ppermute(send, "c", [(0, 1), (1, 0)])
            return (keep.astype(F32) + got.astype(F32)).astype(BF).reshape(8, 1, 128, 256)

        pair = jnp.concatenate([core_sum(row_keep, row_send), core_sum(col_keep, col_send)], axis=1)
        plane = lax.all_to_all(
            pair.reshape(16, 128, 256), ("x", "yh", "yl"), split_axis=0, concat_axis=0, tiled=True
        )
        plane = jnp.sum(plane.astype(F32), axis=0)
        line = lax.all_to_all(
            plane.reshape(16, 8, 256), "z", split_axis=0, concat_axis=0, tiled=True
        )
        line = jnp.sum(line, axis=0)
        last = lax.all_to_all(
            line.reshape(4, 2, 256), ("yl", "c"), split_axis=0, concat_axis=0, tiled=True
        ).reshape(2, 2, 2, 256)
        grad_value = jnp.transpose(last[:, 0], (1, 0, 2)).reshape(2, 512)
        grad_output = jnp.transpose(last[:, 1], (0, 2, 1)).reshape(512, 2)
    mixed, grad_tokens = final_call(core_arg, row_parts, returned, own, other)
    return (
        mixed.reshape(tokens.shape),
        grad_tokens.reshape(tokens.shape),
        grad_value,
        grad_output,
    )


def solution(mesh):
    fine = Mesh(mesh.devices.reshape(4, 2, 16, 2, 2), ("x", "yh", "z", "yl", "c"))
    dp, seq = ("x", "yh"), ("z", "yl", "c")
    return jax.shard_map(
        body,
        mesh=fine,
        in_specs=(
            P(dp, seq, None, None),
            P(dp, seq, None, None),
            P(None, seq, None, None),
            P(None, seq, None, None),
            P(dp, None),
            P(dp, None),
            P(dp, None),
            P(dp, None),
        ),
        out_specs=(
            P(dp, seq, None, None),
            P(dp, seq, None, None),
            P(dp + seq, None),
            P(None, dp + seq),
        ),
        check_vma=False,
    )
```

```python
import functools

import jax
import jax.numpy as jnp
from jax import lax
from jax.experimental import pallas as pl
from jax.experimental.pallas import tpu as pltpu
from jax.sharding import Mesh, PartitionSpec as P

HEAD_DIM = 64
ROWBLK = 128
COLBLK = 8
BF = jnp.bfloat16
F32 = jnp.float32
LAST = (((1,), (1,)), ((), ()))
FIRST = (((0,), (0,)), ((), ()))
MASKED = -1e30
VMEM = pl.BlockSpec(memory_space=pltpu.VMEM)
SMEM = pl.BlockSpec(memory_space=pltpu.SMEM)
ANYWHERE = pl.BlockSpec(memory_space=pl.ANY)
PARAMS = pltpu.CompilerParams(vmem_limit_bytes=24 * 1024 * 1024)
OFFSETS = [(dx, dy) for dx in range(4) for dy in range(2)]
SWAP = [(0, 1), (1, 0)]


def product(a, b, dims=(((1,), (0,)), ((), ()))):
    return lax.dot_general(a, b, dims, preferred_element_type=F32)


def eights(first):
    row = lax.broadcasted_iota(jnp.int32, (512, 256), 0)
    col = lax.broadcasted_iota(jnp.int32, (512, 256), 1)
    inside = (row & 4) == (0 if first else 4)
    return ((col == (row >> 3) * 4 + (row & 3)) & inside).astype(F32).astype(BF)


def interleave(first, second):
    return (product(eights(True), first) + product(eights(False), second)).astype(BF)


def separate(both):
    return tuple(product(eights(t), both, FIRST).astype(BF) for t in (True, False))


def start_copies(pairs, sems, first=0):
    copies = [
        pltpu.make_async_copy(source, target, sems.at[first + i])
        for i, (source, target) in enumerate(pairs)
    ]
    for copy in copies:
        copy.start()
    return copies


def wait_for(copies):
    for copy in copies:
        copy.wait()


def prepare_kernel(
    place, x_ref, ct_ref, wq_ref, wk_ref, wv_ref, wo_ref, packed_ref, sent_ref, x, ct, sems
):
    core = place[0]
    here = pl.ds(pl.multiple_of(core * 256, 256), 256)
    pairs = [(x_ref, x), (ct_ref, ct)]
    for i, ref in enumerate((wq_ref, wk_ref, wv_ref)):
        pairs.append((ref.at[:, here], packed_ref.at[:, pl.ds(i * 256, 256)]))
    for b in range(2):
        there = pl.ds(pl.multiple_of(core * 512 + b * 256, 256), 256)
        pairs.append((wo_ref.at[:, there], packed_ref.at[pl.ds(b * 64, 64), pl.ds(768, 256)]))
    copies = start_copies(pairs, sems)
    wait_for(copies[:2])
    sent_ref[...] = interleave(x[...], ct[...])
    wait_for(copies[2:])


def attention(x, ct, weights, kind, bias_ref):
    qkv = product(x, weights[kind, :, :, 0:768].reshape(1024, 768)).astype(BF)
    q, k, v = qkv[:, :256], qkv[:, 256:512], qkv[:, 512:]
    do = jnp.zeros((256, 256), F32)
    for half in range(2):
        for b in range(2):
            block = weights[half, kind * 4 : kind * 4 + 4, b * 64 : (b + 1) * 64, 768:1024]
            start = half * 512 + b * 256
            do += product(ct[:, start : start + 256], block.reshape(256, 256), LAST)
    do = do.astype(BF)
    lane = lax.broadcasted_iota(jnp.int32, (256, 256), 1) // HEAD_DIM
    zero = jnp.zeros_like(q)
    out = jnp.zeros((256, 256), F32)
    dq, dk, dv = out, out, out
    for h in range(4):
        mine = lane == h
        kh, vh = jnp.where(mine, k, zero), jnp.where(mine, v, zero)
        qh, doh = jnp.where(mine, q, zero), jnp.where(mine, do, zero)
        s = product(q, kh, LAST) * 0.125 + bias_ref[h].astype(F32)
        e = jnp.exp(s - jnp.max(s, axis=-1, keepdims=True))
        w = e * (1.0 / jnp.sum(e, axis=-1, keepdims=True))
        p = w.astype(BF)
        out += product(p, vh)
        dp = product(do, vh, LAST).astype(BF).astype(F32)
        ds = (w * (dp - jnp.sum(dp * w, axis=-1, keepdims=True)) * 0.125).astype(BF)
        dq += product(ds, kh)
        dk += product(ds, qh, FIRST)
        dv += product(p, doh, FIRST)
    return tuple(a.astype(BF) for a in (out, dq, dk, dv))


def store_gradients(core, x, ct, out, dv, keep_ref, send_ref):
    grad_value = product(x, dv, FIRST).astype(BF)
    grad_out = product(ct, out, FIRST).astype(BF)

    @pl.when(core == 0)
    def _():
        keep_ref[...] = grad_value
        send_ref[...] = grad_out

    @pl.when(core != 0)
    def _():
        keep_ref[...] = grad_out
        send_ref[...] = grad_value


def row_kernel(
    place,
    x_ref,
    ct_ref,
    bias_ref,
    own_ref,
    other_ref,
    parts_ref,
    keep_ref,
    send_ref,
    w_ref,
    x_here,
    ct_here,
    bias,
    sems,
):
    core = place[0]
    pairs = []
    for index, (dx, dy) in enumerate(OFFSETS):
        source = ((place[1] + 4 - dx) & 3) * 2 + ((place[2] + dy) & 1)
        for half, ref in ((core, own_ref), (1 - core, other_ref)):
            pairs.append((ref.at[index], w_ref.at[half, source]))
    pairs += [(x_ref, x_here), (ct_ref, ct_here), (bias_ref, bias)]
    wait_for(start_copies(pairs, sems))
    x, ct = x_here[...], ct_here[...]
    out, dq, dk, dv = attention(x, ct, w_ref, 0, bias)
    for i, part in enumerate((out, dq, dk, dv)):
        parts_ref[:, i * 256 : (i + 1) * 256] = part
    store_gradients(core, x, ct, out, dv, keep_ref, send_ref)


def column_kernel(
    place, both_ref, bias_ref, w_ref, parts_ref, keep_ref, send_ref, both, bias, weights, sems
):
    copies = start_copies(((both_ref, both), (w_ref, weights), (bias_ref, bias)), sems)
    wait_for(copies[:1])
    x, ct = separate(both[...])
    wait_for(copies[1:])
    out, dq, dk, dv = attention(x, ct, weights, 1, bias)
    parts_ref[...] = interleave(
        jnp.concatenate([out, dq], axis=1), jnp.concatenate([dk, dv], axis=1)
    )
    store_gradients(place[0], x, ct, out, dv, keep_ref, send_ref)


def final_kernel(row_ref, col_ref, weights, mixed_ref, gt_ref, row, col, w_ref, sems):
    copies = start_copies(((col_ref, col), (row_ref, row), (weights, w_ref)), sems)
    wait_for(copies[:2])
    first, second = separate(col[...])
    wait_for(copies[2:])
    sides = (
        (row[:, 0:256], row[:, 256:1024]),
        (first[:, 0:256], jnp.concatenate([first[:, 256:512], second], axis=1)),
    )
    for half in range(2):
        for b in range(2):
            total = jnp.zeros((256, 256), F32)
            for kind in range(2):
                block = w_ref[half, kind * 4 : kind * 4 + 4, b * 64 : (b + 1) * 64, 768:1024]
                total += product(sides[kind][0], block.reshape(256, 256))
            start = half * 512 + b * 256
            mixed_ref[:, start : start + 256] = total.astype(BF)
    total = jnp.zeros(gt_ref.shape, F32)
    for kind in range(2):
        total += product(sides[kind][1], w_ref[kind, :, :, 0:768].reshape(1024, 768), LAST)
    gt_ref[...] = total.astype(BF)


def shape(*dims):
    return jax.ShapeDtypeStruct(dims, BF)


def buffer(*dims):
    return pltpu.VMEM(dims, BF)


def cost(flops, moved):
    return pl.CostEstimate(flops=flops, bytes_accessed=moved, transcendentals=0)


def one_hot(index, size):
    return (index[:, None] == jnp.arange(size)[None, :]).astype(BF)


def biases(row_mask, column_mask):
    position = jnp.arange(256)
    seen = position[:, None] >= position[None, :]
    row_in = one_hot(position // ROWBLK, 2)
    row_blocks = jnp.einsum(
        "ia,hab,jb->hij", row_in, row_mask[:, 0].astype(BF), row_in, preferred_element_type=BF
    )
    same = (position[:, None] % 4) == (position[None, :] % 4)
    col_left = one_hot((position % 4) * 8 + position // (4 * COLBLK), 32)
    col_right = one_hot(position // (4 * COLBLK), 8)
    col_blocks = jnp.einsum(
        "ia,hab,jb->hij",
        col_left,
        column_mask.reshape(4, 32, 8).astype(BF),
        col_right,
        preferred_element_type=BF,
    )
    row_bias = jnp.where((row_blocks > 0.5) & seen, 0.0, MASKED).astype(BF)
    col_bias = jnp.where((col_blocks > 0.5) & seen & same, 0.0, MASKED).astype(BF)
    return row_bias, col_bias


def shifted(dx, dy):
    return [
        (x * 2 + y, (x + dx) % 4 * 2 + (y + dy) % 2) for x in range(4) for y in range(2)
    ]


def body(tokens, cotangent, row_mask, column_mask, w_query, w_key, w_value, w_out):
    core, across, high, low = (lax.axis_index(name) for name in ("c", "x", "yh", "yl"))
    place = jnp.stack([core, across, high]).astype(jnp.int32)
    flat = tokens.reshape(256, 1024)
    cot_flat = cotangent.reshape(256, 1024)
    seq = ("z", "yl", "c")

    packed, sent = pl.pallas_call(
        prepare_kernel,
        out_shape=(shape(128, 1024), shape(512, 1024)),
        in_specs=[SMEM] + [ANYWHERE] * 6,
        out_specs=(VMEM, VMEM),
        scratch_shapes=[buffer(256, 1024), buffer(256, 1024), pltpu.SemaphoreType.DMA((7,))],
        compiler_params=PARAMS,
        cost_estimate=cost(540000000, 4000000),
        name="prepare",
    )(place, flat, cot_flat, w_query, w_key, w_value, w_out)
    with jax.named_scope("to_columns"):
        both = lax.all_to_all(
            sent.reshape(64, 8, 1024), seq, split_axis=0, concat_axis=0, tiled=True
        ).reshape(512, 1024)
    with jax.named_scope("weights"):
        own = jnp.stack(
            [packed]
            + [lax.ppermute(packed, ("x", "yh"), shifted(dx, dy)) for dx, dy in OFFSETS[1:]]
        )
        other = lax.ppermute(own, "c", SWAP)
    with jax.named_scope("masks"):
        row_bias, col_bias = biases(row_mask, column_mask)
    row_parts, row_keep, row_send, weights = pl.pallas_call(
        row_kernel,
        out_shape=(shape(256, 1024), shape(1024, 256), shape(1024, 256), shape(2, 8, 128, 1024)),
        in_specs=[SMEM] + [ANYWHERE] * 5,
        out_specs=(VMEM,) * 4,
        scratch_shapes=[
            buffer(256, 1024),
            buffer(256, 1024),
            buffer(4, 256, 256),
            pltpu.SemaphoreType.DMA((19,)),
        ],
        compiler_params=PARAMS,
        cost_estimate=cost(1400000000, 12000000),
        name="row_heads",
    )(place, flat, cot_flat, row_bias, own, other)
    col_parts, col_keep, col_send = pl.pallas_call(
        column_kernel,
        out_shape=(shape(512, 512), shape(1024, 256), shape(1024, 256)),
        in_specs=[SMEM] + [ANYWHERE] * 3,
        out_specs=(VMEM,) * 3,
        scratch_shapes=[
            buffer(512, 1024),
            buffer(4, 256, 256),
            buffer(2, 8, 128, 1024),
            pltpu.SemaphoreType.DMA((3,)),
        ],
        compiler_params=PARAMS,
        cost_estimate=cost(1900000000, 8000000),
        name="column_heads",
    )(place, both, col_bias, weights)
    with jax.named_scope("from_columns"):
        returned = lax.all_to_all(
            col_parts.reshape(64, 8, 512), seq, split_axis=0, concat_axis=0, tiled=True
        ).reshape(512, 512)

    def plane_sum(keep, send):
        got = lax.ppermute(send, "c", SWAP)
        held = (keep.astype(F32) + got.astype(F32)).astype(BF)

        def rows_of(step):
            return lax.dynamic_slice_in_dim(held, ((across + step) & 3) * 256, 256, axis=0)

        terms = [rows_of(0)]
        for step in (1, 3, 2):
            pairs = [(x, (x + step) % 4) for x in range(4)]
            terms.append(lax.ppermute(rows_of(step), "x", pairs))
        held_rows = sum(term.astype(F32) for term in terms).astype(BF)

        def block_of(dh, dl):
            return lax.dynamic_slice(held_rows, ((high ^ dh) * 128, (low ^ dl) * 128), (128, 128))

        terms = [block_of(0, 0)]
        for dh, dl in ((0, 1), (1, 0), (1, 1)):
            pairs = [(h * 2 + l, (h ^ dh) * 2 + (l ^ dl)) for h in range(2) for l in range(2)]
            terms.append(lax.ppermute(block_of(dh, dl), ("yh", "yl"), pairs))
        return sum(term.astype(F32) for term in terms)

    with jax.named_scope("gradient_sums"):
        plane = jnp.concatenate([plane_sum(row_keep, row_send), plane_sum(col_keep, col_send)], axis=1)
        plane, returned = lax.optimization_barrier((plane, returned))
        line = lax.all_to_all(
            plane.reshape(64, 2, 256), seq, split_axis=0, concat_axis=0, tiled=True
        )
        line = jnp.sum(line.reshape(16, 2, 2, 2, 2, 128), axis=0)
        grad_value = jnp.transpose(line[:, 0], (1, 2, 0, 3)).reshape(2, 512)
        grad_output = jnp.transpose(line[:, 1], (2, 0, 3, 1)).reshape(512, 2)
    mixed, grad_tokens = pl.pallas_call(
        final_kernel,
        out_shape=(shape(256, 1024), shape(256, 1024)),
        in_specs=[ANYWHERE] * 3,
        out_specs=(VMEM, VMEM),
        scratch_shapes=[
            buffer(256, 1024),
            buffer(512, 512),
            buffer(2, 8, 128, 1024),
            pltpu.SemaphoreType.DMA((3,)),
        ],
        compiler_params=PARAMS,
        cost_estimate=cost(1200000000, 8000000),
        name="output_products",
    )(row_parts, returned, weights)
    return (
        mixed.reshape(tokens.shape),
        grad_tokens.reshape(tokens.shape),
        grad_value,
        grad_output,
    )


def solution(mesh):
    fine = Mesh(mesh.devices.reshape(4, 2, 16, 2, 2), ("x", "yh", "z", "yl", "c"))
    dp, seq = ("x", "yh"), ("z", "yl", "c")
    return jax.shard_map(
        body,
        mesh=fine,
        in_specs=(
            P(dp, seq, None, None),
            P(dp, seq, None, None),
            P(None, seq, None, None),
            P(None, seq, None, None),
            P(dp, None),
            P(dp, None),
            P(dp, None),
            P(dp, None),
        ),
        out_specs=(
            P(dp, seq, None, None),
            P(dp, seq, None, None),
            P(dp + seq, None),
            P(None, dp + seq),
        ),
        check_vma=False,
    )
```

```python
import functools

import jax
import jax.numpy as jnp
from jax import lax
from jax.experimental import pallas as pl
from jax.experimental.pallas import tpu as pltpu
from jax.sharding import Mesh, PartitionSpec as P

HEAD_DIM = 64
ROWBLK = 128
COLBLK = 8
BF = jnp.bfloat16
F32 = jnp.float32
LAST = (((1,), (1,)), ((), ()))
FIRST = (((0,), (0,)), ((), ()))
MASKED = -1e30
VMEM = pl.BlockSpec(memory_space=pltpu.VMEM)
SMEM = pl.BlockSpec(memory_space=pltpu.SMEM)
ANYWHERE = pl.BlockSpec(memory_space=pl.ANY)
PARAMS = pltpu.CompilerParams(vmem_limit_bytes=60 * 1024 * 1024)
OFFSETS = [(dx, dy) for dx in range(4) for dy in range(2)]
SWAP = [(0, 1), (1, 0)]


def product(a, b, dims=(((1,), (0,)), ((), ()))):
    return lax.dot_general(a, b, dims, preferred_element_type=F32)


def eights(first):
    row = lax.broadcasted_iota(jnp.int32, (512, 256), 0)
    col = lax.broadcasted_iota(jnp.int32, (512, 256), 1)
    inside = (row & 4) == (0 if first else 4)
    return ((col == (row >> 3) * 4 + (row & 3)) & inside).astype(F32).astype(BF)


def interleave(first, second):
    return (product(eights(True), first) + product(eights(False), second)).astype(BF)


def separate(both):
    return tuple(product(eights(t), both, FIRST).astype(BF) for t in (True, False))


def start_copies(pairs, sems, first=0):
    copies = [
        pltpu.make_async_copy(source, target, sems.at[first + i])
        for i, (source, target) in enumerate(pairs)
    ]
    for copy in copies:
        copy.start()
    return copies


def wait_for(copies):
    for copy in copies:
        copy.wait()


def interleave_kernel(x_ref, ct_ref, sent_ref, x, ct, sems):
    wait_for(start_copies(((x_ref, x), (ct_ref, ct)), sems))
    sent_ref[...] = interleave(x[...], ct[...])


def pack_kernel(place, wq_ref, wk_ref, wv_ref, wo_ref, after_ref, packed_ref, sems):
    del after_ref
    core = place[0]
    here = pl.ds(pl.multiple_of(core * 256, 256), 256)
    pairs = []
    for i, ref in enumerate((wq_ref, wk_ref, wv_ref)):
        pairs.append((ref.at[:, here], packed_ref.at[:, pl.ds(i * 256, 256)]))
    for b in range(2):
        there = pl.ds(pl.multiple_of(core * 512 + b * 256, 256), 256)
        pairs.append((wo_ref.at[:, there], packed_ref.at[pl.ds(b * 64, 64), pl.ds(768, 256)]))
    wait_for(start_copies(pairs, sems))


def attention(x, ct, weights, kind, bias_ref):
    qkv = product(x, weights[kind, :, :, 0:768].reshape(1024, 768)).astype(BF)
    q, k, v = qkv[:, :256], qkv[:, 256:512], qkv[:, 512:]
    do = jnp.zeros((256, 256), F32)
    for half in range(2):
        for b in range(2):
            block = weights[half, kind * 4 : kind * 4 + 4, b * 64 : (b + 1) * 64, 768:1024]
            start = half * 512 + b * 256
            do += product(ct[:, start : start + 256], block.reshape(256, 256), LAST)
    do = do.astype(BF)
    lane = lax.broadcasted_iota(jnp.int32, (256, 256), 1) // HEAD_DIM
    zero = jnp.zeros_like(q)
    out = jnp.zeros((256, 256), F32)
    dq, dk, dv = out, out, out
    for h in range(4):
        mine = lane == h
        kh, vh = jnp.where(mine, k, zero), jnp.where(mine, v, zero)
        qh, doh = jnp.where(mine, q, zero), jnp.where(mine, do, zero)
        s = product(q, kh, LAST) * 0.125 + bias_ref[h].astype(F32)
        e = jnp.exp(s - jnp.max(s, axis=-1, keepdims=True))
        w = e * (1.0 / jnp.sum(e, axis=-1, keepdims=True))
        p = w.astype(BF)
        out += product(p, vh)
        dp = product(do, vh, LAST).astype(BF).astype(F32)
        ds = (w * (dp - jnp.sum(dp * w, axis=-1, keepdims=True)) * 0.125).astype(BF)
        dq += product(ds, kh)
        dk += product(ds, qh, FIRST)
        dv += product(p, doh, FIRST)
    return tuple(a.astype(BF) for a in (out, dq, dk, dv))


def store_gradients(core, x, ct, out, dv, keep_ref, send_ref):
    gradients = jnp.concatenate(
        [product(x, dv, FIRST).astype(BF), product(ct, out, FIRST).astype(BF)], axis=1
    )
    new = lax.broadcasted_iota(jnp.int32, (128, 128), 0)
    old = lax.broadcasted_iota(jnp.int32, (128, 128), 1)
    source = ((new >> 1) & 15) * 8 + ((new >> 5) & 1) * 4 + ((new >> 6) ^ core) * 2 + (new & 1)
    order = (old == source).astype(F32).astype(BF)
    for block in range(8):
        moved = product(order, gradients[block * 128 : (block + 1) * 128]).astype(BF)
        keep_ref[block * 64 : (block + 1) * 64, :] = moved[:64]
        send_ref[block * 64 : (block + 1) * 64, :] = moved[64:]


def row_kernel(
    place,
    x_ref,
    ct_ref,
    bias_ref,
    own_ref,
    other_ref,
    parts_ref,
    keep_ref,
    send_ref,
    w_ref,
    x_here,
    ct_here,
    bias,
    sems,
):
    core = place[0]
    pairs = []
    for index, (dx, dy) in enumerate(OFFSETS):
        source = ((place[1] + 4 - dx) & 3) * 2 + ((place[2] + dy) & 1)
        for half, ref in ((core, own_ref), (1 - core, other_ref)):
            pairs.append((ref.at[index], w_ref.at[half, source]))
    pairs += [(x_ref, x_here), (ct_ref, ct_here), (bias_ref, bias)]
    wait_for(start_copies(pairs, sems))
    x, ct = x_here[...], ct_here[...]
    out, dq, dk, dv = attention(x, ct, w_ref, 0, bias)
    for i, part in enumerate((out, dq, dk, dv)):
        parts_ref[:, i * 256 : (i + 1) * 256] = part
    store_gradients(core, x, ct, out, dv, keep_ref, send_ref)


def column_kernel(
    place, both_ref, bias_ref, w_ref, parts_ref, keep_ref, send_ref, both, bias, weights, sems
):
    copies = start_copies(((both_ref, both), (w_ref, weights), (bias_ref, bias)), sems)
    wait_for(copies[:1])
    x, ct = separate(both[...])
    wait_for(copies[1:])
    out, dq, dk, dv = attention(x, ct, weights, 1, bias)
    parts_ref[...] = interleave(
        jnp.concatenate([out, dq], axis=1), jnp.concatenate([dk, dv], axis=1)
    )
    store_gradients(place[0], x, ct, out, dv, keep_ref, send_ref)


def final_kernel(row_ref, col_ref, weights, mixed_ref, gt_ref, row, col, w_ref, sems):
    copies = start_copies(((col_ref, col), (row_ref, row), (weights, w_ref)), sems)
    wait_for(copies[:2])
    first, second = separate(col[...])
    wait_for(copies[2:])
    sides = (
        (row[:, 0:256], row[:, 256:1024]),
        (first[:, 0:256], jnp.concatenate([first[:, 256:512], second], axis=1)),
    )
    for half in range(2):
        for b in range(2):
            total = jnp.zeros((256, 256), F32)
            for kind in range(2):
                block = w_ref[half, kind * 4 : kind * 4 + 4, b * 64 : (b + 1) * 64, 768:1024]
                total += product(sides[kind][0], block.reshape(256, 256))
            start = half * 512 + b * 256
            mixed_ref[:, start : start + 256] = total.astype(BF)
    total = jnp.zeros(gt_ref.shape, F32)
    for kind in range(2):
        total += product(sides[kind][1], w_ref[kind, :, :, 0:768].reshape(1024, 768), LAST)
    gt_ref[...] = total.astype(BF)


def shape(*dims):
    return jax.ShapeDtypeStruct(dims, BF)


def buffer(*dims):
    return pltpu.VMEM(dims, BF)


def cost(flops, moved):
    return pl.CostEstimate(flops=flops, bytes_accessed=moved, transcendentals=0)


def one_hot(index, size):
    return (index[:, None] == jnp.arange(size)[None, :]).astype(BF)


def biases(row_mask, column_mask):
    position = jnp.arange(256)
    seen = position[:, None] >= position[None, :]
    row_in = one_hot(position // ROWBLK, 2)
    row_blocks = jnp.einsum(
        "ia,hab,jb->hij", row_in, row_mask[:, 0].astype(BF), row_in, preferred_element_type=BF
    )
    same = (position[:, None] % 4) == (position[None, :] % 4)
    col_left = one_hot((position % 4) * 8 + position // (4 * COLBLK), 32)
    col_right = one_hot(position // (4 * COLBLK), 8)
    col_blocks = jnp.einsum(
        "ia,hab,jb->hij",
        col_left,
        column_mask.reshape(4, 32, 8).astype(BF),
        col_right,
        preferred_element_type=BF,
    )
    row_bias = jnp.where((row_blocks > 0.5) & seen, 0.0, MASKED).astype(BF)
    col_bias = jnp.where((col_blocks > 0.5) & seen & same, 0.0, MASKED).astype(BF)
    return row_bias, col_bias


def shifted(dx, dy):
    return [
        (x * 2 + y, (x + dx) % 4 * 2 + (y + dy) % 2) for x in range(4) for y in range(2)
    ]


def body(tokens, cotangent, row_mask, column_mask, w_query, w_key, w_value, w_out):
    core, across, high, low = (lax.axis_index(name) for name in ("c", "x", "yh", "yl"))
    place = jnp.stack([core, across, high]).astype(jnp.int32)
    flat = tokens.reshape(256, 1024)
    cot_flat = cotangent.reshape(256, 1024)
    seq = ("z", "yl", "c")

    sent = pl.pallas_call(
        interleave_kernel,
        out_shape=shape(512, 1024),
        in_specs=[ANYWHERE] * 2,
        out_specs=VMEM,
        scratch_shapes=[buffer(256, 1024), buffer(256, 1024), pltpu.SemaphoreType.DMA((2,))],
        compiler_params=PARAMS,
        cost_estimate=cost(540000000, 2000000),
        name="interleave",
    )(flat, cot_flat)
    packed = pl.pallas_call(
        pack_kernel,
        out_shape=shape(128, 1024),
        in_specs=[SMEM] + [ANYWHERE] * 5,
        out_specs=VMEM,
        scratch_shapes=[pltpu.SemaphoreType.DMA((5,))],
        compiler_params=PARAMS,
        cost_estimate=cost(90000000000, 2000000),
        name="pack",
    )(place, w_query, w_key, w_value, w_out, sent)
    with jax.named_scope("to_columns"):
        both = lax.all_to_all(
            sent.reshape(64, 8, 1024), seq, split_axis=0, concat_axis=0, tiled=True
        ).reshape(512, 1024)
    with jax.named_scope("weights"):
        own = jnp.stack(
            [packed]
            + [lax.ppermute(packed, ("x", "yh"), shifted(dx, dy)) for dx, dy in OFFSETS[1:]]
        )
        other = lax.ppermute(own, "c", SWAP)
    with jax.named_scope("masks"):
        row_bias, col_bias = biases(row_mask, column_mask)
    row_parts, row_keep, row_send, weights = pl.pallas_call(
        row_kernel,
        out_shape=(shape(256, 1024), shape(512, 512), shape(512, 512), shape(2, 8, 128, 1024)),
        in_specs=[SMEM] + [ANYWHERE] * 5,
        out_specs=(VMEM,) * 4,
        scratch_shapes=[
            buffer(256, 1024),
            buffer(256, 1024),
            buffer(4, 256, 256),
            pltpu.SemaphoreType.DMA((19,)),
        ],
        compiler_params=PARAMS,
        cost_estimate=cost(1400000000, 12000000),
        name="row_heads",
    )(place, flat, cot_flat, row_bias, own, other)
    col_parts, col_keep, col_send = pl.pallas_call(
        column_kernel,
        out_shape=(shape(512, 512),) * 3,
        in_specs=[SMEM] + [ANYWHERE] * 3,
        out_specs=(VMEM,) * 3,
        scratch_shapes=[
            buffer(512, 1024),
            buffer(4, 256, 256),
            buffer(2, 8, 128, 1024),
            pltpu.SemaphoreType.DMA((3,)),
        ],
        compiler_params=PARAMS,
        cost_estimate=cost(1900000000, 8000000),
        name="column_heads",
    )(place, both, col_bias, weights)
    with jax.named_scope("from_columns"):
        returned = lax.all_to_all(
            col_parts.reshape(64, 8, 512), seq, split_axis=0, concat_axis=0, tiled=True
        ).reshape(512, 512)

    def core_sum(keep, send):
        got = lax.ppermute(send, "c", SWAP)
        return (keep.astype(F32) + got.astype(F32)).astype(BF)

    def plane_sum(held):
        def x_rows(step):
            return lax.dynamic_slice_in_dim(held, ((across + step) & 3) * 128, 128, axis=0)

        terms = [x_rows(0)]
        for step in (1, 3, 2):
            pairs = [(x, (x + step) % 4) for x in range(4)]
            terms.append(lax.ppermute(x_rows(step), "x", pairs))
        line = sum(term.astype(F32) for term in terms).astype(BF)
        mine = high * 2 + low
        terms = [lax.dynamic_slice_in_dim(line, mine * 32, 32, axis=0)]
        for step in (1, 2, 3):
            pairs = [(y, y ^ step) for y in range(4)]
            rows = lax.dynamic_slice_in_dim(line, (mine ^ step) * 32, 32, axis=0)
            terms.append(lax.ppermute(rows, ("yh", "yl"), pairs))
        return sum(term.astype(F32) for term in terms)

    with jax.named_scope("gradient_sums"):
        held = jnp.concatenate([core_sum(row_keep, row_send), core_sum(col_keep, col_send)], axis=1)
        plane = plane_sum(held)
        plane, returned = lax.optimization_barrier((plane, returned))
        line = lax.all_to_all(
            plane.reshape(16, 2, 1024), "z", split_axis=0, concat_axis=0, tiled=True
        )
        line = jnp.sum(line, axis=0)
        grad_value = jnp.concatenate([line[:, 0:256], line[:, 512:768]], axis=1)
        grad_output = jnp.transpose(
            jnp.concatenate([line[:, 256:512], line[:, 768:1024]], axis=1)
        )
    mixed, grad_tokens = pl.pallas_call(
        final_kernel,
        out_shape=(shape(256, 1024), shape(256, 1024)),
        in_specs=[ANYWHERE] * 3,
        out_specs=(VMEM, VMEM),
        scratch_shapes=[
            buffer(256, 1024),
            buffer(512, 512),
            buffer(2, 8, 128, 1024),
            pltpu.SemaphoreType.DMA((3,)),
        ],
        compiler_params=PARAMS,
        cost_estimate=cost(1200000000, 8000000),
        name="output_products",
    )(row_parts, returned, weights)
    return (
        mixed.reshape(tokens.shape),
        grad_tokens.reshape(tokens.shape),
        grad_value,
        grad_output,
    )


def solution(mesh):
    fine = Mesh(mesh.devices.reshape(4, 2, 16, 2, 2), ("x", "yh", "z", "yl", "c"))
    dp, seq = ("x", "yh"), ("z", "yl", "c")
    return jax.shard_map(
        body,
        mesh=fine,
        in_specs=(
            P(dp, seq, None, None),
            P(dp, seq, None, None),
            P(None, seq, None, None),
            P(None, seq, None, None),
            P(dp, None),
            P(dp, None),
            P(dp, None),
            P(dp, None),
        ),
        out_specs=(
            P(dp, seq, None, None),
            P(dp, seq, None, None),
            P(dp + seq, None),
            P(None, dp + seq),
        ),
        check_vma=False,
    )
```

```python
import functools

import jax
import jax.numpy as jnp
from jax import lax
from jax.experimental import pallas as pl
from jax.experimental.pallas import tpu as pltpu
from jax.sharding import Mesh, PartitionSpec as P

HEAD_DIM = 64
ROWBLK = 128
COLBLK = 8
BF = jnp.bfloat16
F32 = jnp.float32
LAST = (((1,), (1,)), ((), ()))
FIRST = (((0,), (0,)), ((), ()))
MASKED = -1e30
VMEM = pl.BlockSpec(memory_space=pltpu.VMEM)
ANYWHERE = pl.BlockSpec(memory_space=pl.ANY)
PARAMS = pltpu.CompilerParams(vmem_limit_bytes=60 * 1024 * 1024)
STEPS = (0, 1, 3, 2)
SWAP = [(0, 1), (1, 0)]


def product(a, b, dims=(((1,), (0,)), ((), ()))):
    return lax.dot_general(a, b, dims, preferred_element_type=F32)


def eights(first):
    row = lax.broadcasted_iota(jnp.int32, (512, 256), 0)
    col = lax.broadcasted_iota(jnp.int32, (512, 256), 1)
    inside = (row & 4) == (0 if first else 4)
    return ((col == (row >> 3) * 4 + (row & 3)) & inside).astype(F32).astype(BF)


def interleave(first, second):
    return (product(eights(True), first) + product(eights(False), second)).astype(BF)


def separate(both):
    return tuple(product(eights(t), both, FIRST).astype(BF) for t in (True, False))


def start_copies(pairs, sems, first=0):
    copies = [
        pltpu.make_async_copy(source, target, sems.at[first + i])
        for i, (source, target) in enumerate(pairs)
    ]
    for copy in copies:
        copy.start()
    return copies


def wait_for(copies):
    for copy in copies:
        copy.wait()


def interleave_kernel(x_ref, ct_ref, sent_ref, x, ct, sems):
    wait_for(start_copies(((x_ref, x), (ct_ref, ct)), sems))
    sent_ref[...] = interleave(x[...], ct[...])


def pack_kernel(wq_ref, wk_ref, wv_ref, wo_ref, after_ref, packed_ref, sems):
    del after_ref
    core = lax.axis_index("c")
    here = pl.ds(pl.multiple_of(core * 256, 256), 256)
    pairs = []
    for i, ref in enumerate((wq_ref, wk_ref, wv_ref)):
        pairs.append((ref.at[:, here], packed_ref.at[:, pl.ds(i * 256, 256)]))
    for b in range(2):
        there = pl.ds(pl.multiple_of(core * 512 + b * 256, 256), 256)
        pairs.append((wo_ref.at[:, there], packed_ref.at[pl.ds(b * 64, 64), pl.ds(768, 256)]))
    wait_for(start_copies(pairs, sems))


def attention(x, ct, weights, kind, bias_ref):
    qkv = product(x, weights[kind, :, :, 0:768].reshape(1024, 768)).astype(BF)
    q, k, v = qkv[:, :256], qkv[:, 256:512], qkv[:, 512:]
    do = jnp.zeros((256, 256), F32)
    for half in range(2):
        for b in range(2):
            block = weights[half, kind * 4 : kind * 4 + 4, b * 64 : (b + 1) * 64, 768:1024]
            start = half * 512 + b * 256
            do += product(ct[:, start : start + 256], block.reshape(256, 256), LAST)
    do = do.astype(BF)
    lane = lax.broadcasted_iota(jnp.int32, (256, 256), 1) // HEAD_DIM
    zero = jnp.zeros_like(q)
    out = jnp.zeros((256, 256), F32)
    dq, dk, dv = out, out, out
    for h in range(4):
        mine = lane == h
        kh, vh = jnp.where(mine, k, zero), jnp.where(mine, v, zero)
        qh, doh = jnp.where(mine, q, zero), jnp.where(mine, do, zero)
        s = product(q, kh, LAST) * 0.125 + bias_ref[h].astype(F32)
        e = jnp.exp(s - jnp.max(s, axis=-1, keepdims=True))
        w = e * (1.0 / jnp.sum(e, axis=-1, keepdims=True))
        p = w.astype(BF)
        out += product(p, vh)
        dp = product(do, vh, LAST).astype(BF).astype(F32)
        ds = (w * (dp - jnp.sum(dp * w, axis=-1, keepdims=True)) * 0.125).astype(BF)
        dq += product(ds, kh)
        dk += product(ds, qh, FIRST)
        dv += product(p, doh, FIRST)
    return tuple(a.astype(BF) for a in (out, dq, dk, dv))


def store_gradients(core, x, ct, out, dv, keep_ref, send_ref):
    gradients = jnp.concatenate(
        [product(x, dv, FIRST).astype(BF), product(ct, out, FIRST).astype(BF)], axis=1
    )
    new = lax.broadcasted_iota(jnp.int32, (128, 128), 0)
    old = lax.broadcasted_iota(jnp.int32, (128, 128), 1)
    source = ((new >> 1) & 15) * 8 + ((new >> 5) & 1) * 4 + ((new >> 6) ^ core) * 2 + (new & 1)
    order = (old == source).astype(F32).astype(BF)
    for block in range(8):
        moved = product(order, gradients[block * 128 : (block + 1) * 128]).astype(BF)
        keep_ref[block * 64 : (block + 1) * 64, :] = moved[:64]
        send_ref[block * 64 : (block + 1) * 64, :] = moved[64:]


def row_kernel(
    x_ref,
    ct_ref,
    bias_ref,
    own_ref,
    other_ref,
    parts_ref,
    keep_ref,
    send_ref,
    w_ref,
    x_here,
    ct_here,
    bias,
    sems,
):
    core = lax.axis_index("c")
    pairs = []
    across, high = lax.axis_index("x"), lax.axis_index("yh")
    for index, step in enumerate(STEPS):
        for flip in range(2):
            source = ((across + 4 - step) & 3) * 2 + (high ^ flip)
            for half, ref in ((core, own_ref), (1 - core, other_ref)):
                pairs.append((ref.at[index * 2 + flip], w_ref.at[half, source]))
    pairs += [(x_ref, x_here), (ct_ref, ct_here), (bias_ref, bias)]
    wait_for(start_copies(pairs, sems))
    x, ct = x_here[...], ct_here[...]
    out, dq, dk, dv = attention(x, ct, w_ref, 0, bias)
    for i, part in enumerate((out, dq, dk, dv)):
        parts_ref[:, i * 256 : (i + 1) * 256] = part
    store_gradients(core, x, ct, out, dv, keep_ref, send_ref)


def column_kernel(
    both_ref, bias_ref, w_ref, parts_ref, keep_ref, send_ref, both, bias, weights, sems
):
    pairs = [(both_ref, both), (bias_ref, bias)]
    mine, right = pl.ds(0, 768), pl.ds(768, 256)
    pairs.append((w_ref.at[1, :, :, mine], weights.at[1, :, :, mine]))
    for half in range(2):
        wanted = (half, pl.ds(4, 4), slice(None), right)
        pairs.append((w_ref.at[wanted], weights.at[wanted]))
    copies = start_copies(pairs, sems)
    wait_for(copies[:1])
    x, ct = separate(both[...])
    wait_for(copies[1:])
    out, dq, dk, dv = attention(x, ct, weights, 1, bias)
    parts_ref[...] = interleave(
        jnp.concatenate([out, dq], axis=1), jnp.concatenate([dk, dv], axis=1)
    )
    store_gradients(lax.axis_index("c"), x, ct, out, dv, keep_ref, send_ref)


def final_kernel(row_ref, col_ref, weights, mixed_ref, gt_ref, row, col, w_ref, sems):
    copies = start_copies(((col_ref, col), (row_ref, row), (weights, w_ref)), sems)
    wait_for(copies[:2])
    first, second = separate(col[...])
    wait_for(copies[2:])
    sides = (
        (row[:, 0:256], row[:, 256:1024]),
        (first[:, 0:256], jnp.concatenate([first[:, 256:512], second], axis=1)),
    )
    for half in range(2):
        for b in range(2):
            total = jnp.zeros((256, 256), F32)
            for kind in range(2):
                block = w_ref[half, kind * 4 : kind * 4 + 4, b * 64 : (b + 1) * 64, 768:1024]
                total += product(sides[kind][0], block.reshape(256, 256))
            start = half * 512 + b * 256
            mixed_ref[:, start : start + 256] = total.astype(BF)
    total = jnp.zeros(gt_ref.shape, F32)
    for kind in range(2):
        total += product(sides[kind][1], w_ref[kind, :, :, 0:768].reshape(1024, 768), LAST)
    gt_ref[...] = total.astype(BF)


def shape(*dims):
    return jax.ShapeDtypeStruct(dims, BF)


def buffer(*dims):
    return pltpu.VMEM(dims, BF)


def cost(flops, moved):
    return pl.CostEstimate(flops=flops, bytes_accessed=moved, transcendentals=0)


def one_hot(index, size):
    return (index[:, None] == jnp.arange(size)[None, :]).astype(BF)


def biases(row_mask, column_mask):
    position = jnp.arange(256)
    seen = position[:, None] >= position[None, :]
    row_in = one_hot(position // ROWBLK, 2)
    row_blocks = jnp.einsum(
        "ia,hab,jb->hij", row_in, row_mask[:, 0].astype(BF), row_in, preferred_element_type=BF
    )
    same = (position[:, None] % 4) == (position[None, :] % 4)
    col_left = one_hot((position % 4) * 8 + position // (4 * COLBLK), 32)
    col_right = one_hot(position // (4 * COLBLK), 8)
    col_blocks = jnp.einsum(
        "ia,hab,jb->hij",
        col_left,
        column_mask.reshape(4, 32, 8).astype(BF),
        col_right,
        preferred_element_type=BF,
    )
    row_bias = jnp.where((row_blocks > 0.5) & seen, 0.0, MASKED).astype(BF)
    col_bias = jnp.where((col_blocks > 0.5) & seen & same, 0.0, MASKED).astype(BF)
    return row_bias, col_bias


def body(tokens, cotangent, row_mask, column_mask, w_query, w_key, w_value, w_out):
    across, high, low = (lax.axis_index(name) for name in ("x", "yh", "yl"))
    flat = tokens.reshape(256, 1024)
    cot_flat = cotangent.reshape(256, 1024)
    seq = ("z", "yl", "c")

    sent = pl.pallas_call(
        interleave_kernel,
        out_shape=shape(512, 1024),
        in_specs=[ANYWHERE] * 2,
        out_specs=VMEM,
        scratch_shapes=[buffer(256, 1024), buffer(256, 1024), pltpu.SemaphoreType.DMA((2,))],
        compiler_params=PARAMS,
        cost_estimate=cost(540000000, 2000000),
        name="interleave",
    )(flat, cot_flat)
    packed = pl.pallas_call(
        pack_kernel,
        out_shape=shape(128, 1024),
        in_specs=[ANYWHERE] * 5,
        out_specs=VMEM,
        scratch_shapes=[pltpu.SemaphoreType.DMA((5,))],
        compiler_params=PARAMS,
        cost_estimate=cost(90000000000, 2000000),
        name="pack",
    )(w_query, w_key, w_value, w_out, sent)
    with jax.named_scope("to_columns"):
        both = lax.all_to_all(
            sent.reshape(64, 8, 1024), seq, split_axis=0, concat_axis=0, tiled=True
        ).reshape(512, 1024)
    with jax.named_scope("weights"):
        flipped = lax.ppermute(packed, ("yh", "yl"), [(y, 3 - y) for y in range(4)])
        pair = jnp.stack([packed, flipped])
        own = jnp.concatenate(
            [pair]
            + [lax.ppermute(pair, "x", [(x, (x + dx) % 4) for x in range(4)]) for dx in STEPS[1:]]
        )
        other = lax.ppermute(own, "c", SWAP)
    with jax.named_scope("masks"):
        row_bias, col_bias = biases(row_mask, column_mask)
    row_parts, row_keep, row_send, weights = pl.pallas_call(
        row_kernel,
        out_shape=(shape(256, 1024), shape(512, 512), shape(512, 512), shape(2, 8, 128, 1024)),
        in_specs=[ANYWHERE] * 5,
        out_specs=(VMEM,) * 4,
        scratch_shapes=[
            buffer(256, 1024),
            buffer(256, 1024),
            buffer(4, 256, 256),
            pltpu.SemaphoreType.DMA((19,)),
        ],
        compiler_params=PARAMS,
        cost_estimate=cost(1400000000, 12000000),
        name="row_heads",
    )(flat, cot_flat, row_bias, own, other)
    col_parts, col_keep, col_send = pl.pallas_call(
        column_kernel,
        out_shape=(shape(512, 512),) * 3,
        in_specs=[ANYWHERE] * 3,
        out_specs=(VMEM,) * 3,
        scratch_shapes=[
            buffer(512, 1024),
            buffer(4, 256, 256),
            buffer(2, 8, 128, 1024),
            pltpu.SemaphoreType.DMA((5,)),
        ],
        compiler_params=PARAMS,
        cost_estimate=cost(1900000000, 8000000),
        name="column_heads",
    )(both, col_bias, weights)
    with jax.named_scope("from_columns"):
        returned = lax.all_to_all(
            col_parts.reshape(64, 8, 512), seq, split_axis=0, concat_axis=0, tiled=True
        ).reshape(512, 512)

    def core_sum(keep, send):
        got = lax.ppermute(send, "c", SWAP)
        return (keep.astype(F32) + got.astype(F32)).astype(BF)

    def plane_sum(held):
        def x_rows(step):
            return lax.dynamic_slice_in_dim(held, ((across + step) & 3) * 128, 128, axis=0)

        terms = [x_rows(0)]
        for step in (1, 3, 2):
            pairs = [(x, (x + step) % 4) for x in range(4)]
            terms.append(lax.ppermute(x_rows(step), "x", pairs))
        line = sum(term.astype(F32) for term in terms).astype(BF)
        mine = high * 2 + low
        terms = [lax.dynamic_slice_in_dim(line, mine * 32, 32, axis=0)]
        for step in (1, 2, 3):
            pairs = [(y, y ^ step) for y in range(4)]
            rows = lax.dynamic_slice_in_dim(line, (mine ^ step) * 32, 32, axis=0)
            terms.append(lax.ppermute(rows, ("yh", "yl"), pairs))
        return sum(term.astype(F32) for term in terms)

    with jax.named_scope("gradient_sums"):
        held = jnp.concatenate([core_sum(row_keep, row_send), core_sum(col_keep, col_send)], axis=1)
        plane = plane_sum(held)
        plane, returned = lax.optimization_barrier((plane, returned))
        line = lax.all_to_all(
            plane.reshape(16, 2, 1024), "z", split_axis=0, concat_axis=0, tiled=True
        )
        line = jnp.sum(line, axis=0)
        grad_value = jnp.concatenate([line[:, 0:256], line[:, 512:768]], axis=1)
        grad_output = jnp.transpose(
            jnp.concatenate([line[:, 256:512], line[:, 768:1024]], axis=1)
        )
    mixed, grad_tokens = pl.pallas_call(
        final_kernel,
        out_shape=(shape(256, 1024), shape(256, 1024)),
        in_specs=[ANYWHERE] * 3,
        out_specs=(VMEM, VMEM),
        scratch_shapes=[
            buffer(256, 1024),
            buffer(512, 512),
            buffer(2, 8, 128, 1024),
            pltpu.SemaphoreType.DMA((3,)),
        ],
        compiler_params=PARAMS,
        cost_estimate=cost(1200000000, 8000000),
        name="output_products",
    )(row_parts, returned, weights)
    return (
        mixed.reshape(tokens.shape),
        grad_tokens.reshape(tokens.shape),
        grad_value,
        grad_output,
    )


def solution(mesh):
    fine = Mesh(mesh.devices.reshape(4, 2, 16, 2, 2), ("x", "yh", "z", "yl", "c"))
    dp, seq = ("x", "yh"), ("z", "yl", "c")
    return jax.shard_map(
        body,
        mesh=fine,
        in_specs=(
            P(dp, seq, None, None),
            P(dp, seq, None, None),
            P(None, seq, None, None),
            P(None, seq, None, None),
            P(dp, None),
            P(dp, None),
            P(dp, None),
            P(dp, None),
        ),
        out_specs=(
            P(dp, seq, None, None),
            P(dp, seq, None, None),
            P(dp + seq, None),
            P(None, dp + seq),
        ),
        check_vma=False,
    )
```

```python
import functools

import jax
import jax.numpy as jnp
from jax import lax
from jax.experimental import pallas as pl
from jax.experimental.pallas import tpu as pltpu
from jax.sharding import Mesh, PartitionSpec as P

HEAD_DIM = 64
ROWBLK = 128
COLBLK = 8
BF = jnp.bfloat16
F32 = jnp.float32
LAST = (((1,), (1,)), ((), ()))
FIRST = (((0,), (0,)), ((), ()))
MASKED = -1e30
VMEM = pl.BlockSpec(memory_space=pltpu.VMEM)
HBM = pl.BlockSpec(memory_space=pltpu.HBM)


def room(mebibytes):
    return pltpu.CompilerParams(vmem_limit_bytes=mebibytes * 1024 * 1024)


SWAP = [(0, 1), (1, 0)]
PACK, PAIR, PICK = 1000000000, 30000000000, 10000000000


def product(a, b, dims=(((1,), (0,)), ((), ()))):
    return lax.dot_general(a, b, dims, preferred_element_type=F32)


def eights(first):
    row = lax.broadcasted_iota(jnp.int32, (512, 256), 0)
    col = lax.broadcasted_iota(jnp.int32, (512, 256), 1)
    inside = (row & 4) == (0 if first else 4)
    return ((col == (row >> 3) * 4 + (row & 3)) & inside).astype(F32).astype(BF)


def interleave(first, second):
    return (product(eights(True), first) + product(eights(False), second)).astype(BF)


def separate(both):
    return tuple(product(eights(t), both, FIRST).astype(BF) for t in (True, False))


def start_copies(pairs, sems, first=0):
    copies = [
        pltpu.make_async_copy(source, target, sems.at[first + i])
        for i, (source, target) in enumerate(pairs)
    ]
    for copy in copies:
        copy.start()
    return copies


def wait_for(copies):
    for copy in copies:
        copy.wait()


def interleave_kernel(x_ref, ct_ref, sent_ref, x, ct, sems):
    wait_for(start_copies(((x_ref, x), (ct_ref, ct)), sems))
    sent_ref[...] = interleave(x[...], ct[...])


def pack_kernel(wq_ref, wk_ref, wv_ref, wo_ref, packed_ref, sems):
    core = lax.axis_index("c")
    here = pl.ds(pl.multiple_of(core * 256, 256), 256)
    pairs = []
    for i, ref in enumerate((wq_ref, wk_ref, wv_ref)):
        pairs.append((ref.at[:, here], packed_ref.at[:, pl.ds(i * 256, 256)]))
    for b in range(2):
        there = pl.ds(pl.multiple_of(core * 512 + b * 256, 256), 256)
        pairs.append((wo_ref.at[:, there], packed_ref.at[pl.ds(b * 64, 64), pl.ds(768, 256)]))
    wait_for(start_copies(pairs, sems))


def pair_kernel(packed_ref, flipped_ref, pair_ref):
    pair_ref[0] = packed_ref[...]
    pair_ref[1] = flipped_ref[...]


def attention(x, ct, weights, kind, bias_ref):
    qkv = product(x, weights[kind, :, :, 0:768].reshape(1024, 768)).astype(BF)
    q, k, v = qkv[:, :256], qkv[:, 256:512], qkv[:, 512:]
    do = jnp.zeros((256, 256), F32)
    for half in range(2):
        for b in range(2):
            block = weights[half, kind * 4 : kind * 4 + 4, b * 64 : (b + 1) * 64, 768:1024]
            start = half * 512 + b * 256
            do += product(ct[:, start : start + 256], block.reshape(256, 256), LAST)
    do = do.astype(BF)
    lane = lax.broadcasted_iota(jnp.int32, (256, 256), 1) // HEAD_DIM
    zero = jnp.zeros_like(q)
    out = jnp.zeros((256, 256), F32)
    dq, dk, dv = out, out, out
    for h in range(4):
        mine = lane == h
        kh, vh = jnp.where(mine, k, zero), jnp.where(mine, v, zero)
        qh, doh = jnp.where(mine, q, zero), jnp.where(mine, do, zero)
        s = product(q, kh, LAST) * 0.125 + bias_ref[h].astype(F32)
        e = jnp.exp(s - jnp.max(s, axis=-1, keepdims=True))
        w = e * (1.0 / jnp.sum(e, axis=-1, keepdims=True))
        p = w.astype(BF)
        out += product(p, vh)
        dp = product(do, vh, LAST).astype(BF).astype(F32)
        ds = (w * (dp - jnp.sum(dp * w, axis=-1, keepdims=True)) * 0.125).astype(BF)
        dq += product(ds, kh)
        dk += product(ds, qh, FIRST)
        dv += product(p, doh, FIRST)
    return tuple(a.astype(BF) for a in (out, dq, dk, dv))


def store_gradients(core, x, ct, out, dv, keep_ref, send_ref):
    gradients = jnp.concatenate(
        [product(x, dv, FIRST).astype(BF), product(ct, out, FIRST).astype(BF)], axis=1
    )
    new = lax.broadcasted_iota(jnp.int32, (128, 128), 0)
    old = lax.broadcasted_iota(jnp.int32, (128, 128), 1)
    source = ((new >> 1) & 31) * 4 + ((new >> 6) ^ core) * 2 + (new & 1)
    order = (old == source).astype(F32).astype(BF)
    for block in range(8):
        moved = product(order, gradients[block * 128 : (block + 1) * 128]).astype(BF)
        keep_ref[block * 64 : (block + 1) * 64, :] = moved[:64]
        send_ref[block * 64 : (block + 1) * 64, :] = moved[64:]


def weight_copies(refs, w_ref, sems, kinds):
    core, across, high = (lax.axis_index(name) for name in ("c", "x", "yh"))
    right = pl.ds(768, 256)
    pairs, sides = [], ([], [])
    for step in range(4):
        for flip in range(2):
            shard = ((across + 4 - step) & 3) * 2 + (high ^ flip)
            for side, ref in enumerate((refs[step], refs[4 + step])):
                half = core ^ side
                if kinds == 2:
                    pairs.append((ref.at[flip], w_ref.at[half, shard]))
                else:
                    pairs.append((ref.at[flip, :, right], w_ref.at[half, shard, :, right]))
                    left = pl.ds(0, 768)
                    sides[side].append((ref.at[flip, :, left], w_ref.at[half, shard, :, left]))
    return pairs, sides


def kind_copies(kind, refs, w_ref, sems, first):
    pairs, sides = weight_copies(refs, w_ref, sems, 1)
    core = lax.axis_index("c")
    for side in range(2):

        @pl.when((core ^ side) == kind)
        def _(side=side):
            start_copies(sides[side], sems, first)

    waits = [
        pltpu.make_async_copy(source, target, sems.at[first + i])
        for i, (source, target) in enumerate(sides[0])
    ]
    return waits + start_copies(pairs, sems, first + 8)


def row_kernel(x_ref, ct_ref, bias_ref, *refs):
    weights, (parts_ref, keep_ref, send_ref, x_here, ct_here, bias, w_ref, sems) = refs[:8], refs[8:]
    copies = start_copies(((x_ref, x_here), (ct_ref, ct_here), (bias_ref, bias)), sems)
    wait_for(kind_copies(0, weights, w_ref, sems, 3) + copies)
    x, ct = x_here[...], ct_here[...]
    out, dq, dk, dv = attention(x, ct, w_ref, 0, bias)
    for i, part in enumerate((out, dq, dk, dv)):
        parts_ref[:, i * 256 : (i + 1) * 256] = part
    store_gradients(lax.axis_index("c"), x, ct, out, dv, keep_ref, send_ref)


def column_kernel(both_ref, bias_ref, *refs):
    weights, (parts_ref, keep_ref, send_ref, bias, w_ref, sems) = refs[:8], refs[8:]
    copies = kind_copies(1, weights, w_ref, sems, 1) + start_copies(((bias_ref, bias),), sems)
    x, ct = separate(both_ref[...])
    wait_for(copies)
    out, dq, dk, dv = attention(x, ct, w_ref, 1, bias)
    parts_ref[...] = interleave(
        jnp.concatenate([out, dq], axis=1), jnp.concatenate([dk, dv], axis=1)
    )
    store_gradients(lax.axis_index("c"), x, ct, out, dv, keep_ref, send_ref)


def pick_kernel(row_keep, row_got, col_keep, col_got, *terms):
    across = lax.axis_index("x")
    for step, term in enumerate(terms):
        rows = pl.ds(pl.multiple_of(((across + step) & 3) * 128, 128), 128)
        for i, (keep, got) in enumerate(((row_keep, row_got), (col_keep, col_got))):
            total = keep[rows, :].astype(F32) + got[rows, :].astype(F32)
            term[:, i * 512 : (i + 1) * 512] = total.astype(BF)


def line_kernel(*refs):
    given, out_ref = refs[:4], refs[4]
    total = sum(ref[...].astype(F32) for ref in given).astype(BF)
    row = lax.broadcasted_iota(jnp.int32, (512, 128), 0)
    col = lax.broadcasted_iota(jnp.int32, (512, 128), 1)
    out = jnp.zeros((512, 256), F32)
    for b in range(4):
        here = (col == (row >> 3) * 2 + (row & 1)) & ((row & 6) == 2 * b)
        out += product(here.astype(F32).astype(BF), total[:, b * 256 : (b + 1) * 256])
    out_ref[...] = out.astype(BF)


def last_kernel(line_ref, value_ref, out_ref):
    total = jnp.sum(line_ref[...].astype(F32).reshape(64, 8, 256), axis=0)
    for kind in range(2):
        value_ref[:, kind * 256 : (kind + 1) * 256] = total[kind * 4 : kind * 4 + 2]
        out_ref[:, kind * 256 : (kind + 1) * 256] = total[kind * 4 + 2 : kind * 4 + 4]


def final_kernel(row_ref, col_ref, *refs):
    weights, (mixed_ref, gt_ref, row, w_ref, sems) = refs[:8], refs[8:]
    copies = start_copies(weight_copies(weights, w_ref, sems, 2)[0] + [(row_ref, row)], sems)
    first, second = separate(col_ref[...])
    wait_for(copies)
    sides = (
        (row[:, 0:256], row[:, 256:1024]),
        (first[:, 0:256], jnp.concatenate([first[:, 256:512], second], axis=1)),
    )
    for half in range(2):
        for b in range(2):
            total = jnp.zeros((256, 256), F32)
            for kind in range(2):
                block = w_ref[half, kind * 4 : kind * 4 + 4, b * 64 : (b + 1) * 64, 768:1024]
                total += product(sides[kind][0], block.reshape(256, 256))
            start = half * 512 + b * 256
            mixed_ref[:, start : start + 256] = total.astype(BF)
    total = jnp.zeros(gt_ref.shape, F32)
    for kind in range(2):
        total += product(sides[kind][1], w_ref[kind, :, :, 0:768].reshape(1024, 768), LAST)
    gt_ref[...] = total.astype(BF)


def shape(*dims):
    return jax.ShapeDtypeStruct(dims, BF)


def buffer(*dims):
    return pltpu.VMEM(dims, BF)


def cost(flops, moved):
    return pl.CostEstimate(flops=flops, bytes_accessed=moved, transcendentals=0)


def one_hot(index, size):
    return (index[:, None] == jnp.arange(size)[None, :]).astype(BF)


def biases(row_mask, column_mask):
    position = jnp.arange(256)
    seen = position[:, None] >= position[None, :]
    row_in = one_hot(position // ROWBLK, 2)
    row_blocks = jnp.einsum(
        "ia,hab,jb->hij", row_in, row_mask[:, 0].astype(BF), row_in, preferred_element_type=BF
    )
    same = (position[:, None] % 4) == (position[None, :] % 4)
    col_left = one_hot((position % 4) * 8 + position // (4 * COLBLK), 32)
    col_right = one_hot(position // (4 * COLBLK), 8)
    col_blocks = jnp.einsum(
        "ia,hab,jb->hij",
        col_left,
        column_mask.reshape(4, 32, 8).astype(BF),
        col_right,
        preferred_element_type=BF,
    )
    row_bias = jnp.where((row_blocks > 0.5) & seen, 0.0, MASKED).astype(BF)
    col_bias = jnp.where((col_blocks > 0.5) & seen & same, 0.0, MASKED).astype(BF)
    return row_bias, col_bias


def body(tokens, cotangent, row_mask, column_mask, w_query, w_key, w_value, w_out):
    flat = tokens.reshape(256, 1024)
    cot_flat = cotangent.reshape(256, 1024)
    seq = ("z", "yl", "c")

    sent = pl.pallas_call(
        interleave_kernel,
        out_shape=shape(512, 1024),
        in_specs=[HBM] * 2,
        out_specs=VMEM,
        scratch_shapes=[buffer(256, 1024), buffer(256, 1024), pltpu.SemaphoreType.DMA((2,))],
        compiler_params=room(60),
        cost_estimate=cost(540000000, 2000000),
        name="interleave",
    )(flat, cot_flat)
    packed = pl.pallas_call(
        pack_kernel,
        out_shape=shape(128, 1024),
        in_specs=[HBM] * 4,
        out_specs=VMEM,
        scratch_shapes=[pltpu.SemaphoreType.DMA((5,))],
        compiler_params=room(60),
        cost_estimate=cost(PACK, 2000000),
        name="pack",
    )(w_query, w_key, w_value, w_out)
    with jax.named_scope("to_columns"):
        both = lax.all_to_all(
            sent.reshape(64, 8, 1024), seq, split_axis=0, concat_axis=0, tiled=True
        ).reshape(512, 1024)
    with jax.named_scope("masks"):
        row_bias, col_bias = biases(row_mask, column_mask)
    with jax.named_scope("weights"):
        flipped = lax.ppermute(packed, ("yh", "yl"), [(y, 3 - y) for y in range(4)])
        pair = pl.pallas_call(
            pair_kernel,
            out_shape=shape(2, 128, 1024),
            in_specs=[VMEM] * 2,
            out_specs=VMEM,
            compiler_params=room(16),
            cost_estimate=cost(PAIR, 1000000),
            name="pair",
        )(packed, flipped)
        weights = [pair] + [
            lax.ppermute(pair, "x", [(x, (x + step) % 4) for x in range(4)]) for step in (1, 2, 3)
        ]
        weights[3], row_bias, col_bias = lax.optimization_barrier((weights[3], row_bias, col_bias))
        weights += [lax.ppermute(part, "c", SWAP) for part in weights]
    row_parts, row_keep, row_send = pl.pallas_call(
        row_kernel,
        out_shape=(shape(256, 1024), shape(512, 512), shape(512, 512)),
        in_specs=[HBM] * 11,
        out_specs=(VMEM,) * 3,
        scratch_shapes=[
            buffer(256, 1024),
            buffer(256, 1024),
            buffer(4, 256, 256),
            buffer(2, 8, 128, 1024),
            pltpu.SemaphoreType.DMA((27,)),
        ],
        compiler_params=room(58),
        cost_estimate=cost(1400000000, 12000000),
        name="row_heads",
    )(flat, cot_flat, row_bias, *weights)
    row_got = lax.ppermute(row_send, "c", SWAP)
    both, row_keep = lax.optimization_barrier((both, row_keep))
    col_parts, col_keep, col_send = pl.pallas_call(
        column_kernel,
        out_shape=(shape(512, 512),) * 3,
        in_specs=[VMEM] + [HBM] * 9,
        out_specs=(VMEM,) * 3,
        scratch_shapes=[
            buffer(4, 256, 256),
            buffer(2, 8, 128, 1024),
            pltpu.SemaphoreType.DMA((25,)),
        ],
        compiler_params=room(58),
        cost_estimate=cost(1900000000, 8000000),
        name="column_heads",
    )(both, col_bias, *weights)
    col_got = lax.ppermute(col_send, "c", SWAP)
    with jax.named_scope("from_columns"):
        returned = lax.all_to_all(
            col_parts.reshape(64, 8, 512), seq, split_axis=0, concat_axis=0, tiled=True
        ).reshape(512, 512)

    with jax.named_scope("gradient_sums"):
        terms = pl.pallas_call(
            pick_kernel,
            out_shape=(shape(128, 1024),) * 4,
            in_specs=[VMEM] * 4,
            out_specs=(VMEM,) * 4,
            compiler_params=room(16),
            cost_estimate=cost(PICK, 3000000),
            name="pick",
        )(row_keep, row_got, col_keep, col_got)
        moved = [
            lax.ppermute(terms[step], "x", [(x, (x + step) % 4) for x in range(4)])
            for step in (1, 2, 3)
        ]
        line = pl.pallas_call(
            line_kernel,
            out_shape=shape(512, 256),
            in_specs=[VMEM] * 4,
            out_specs=VMEM,
            compiler_params=room(16),
            cost_estimate=cost(10000000, 300000),
            name="line",
        )(terms[0], *moved)
        line, returned = lax.optimization_barrier((line, returned))
        line = lax.all_to_all(
            line.reshape(64, 8, 256), ("yh", "z", "yl"), split_axis=0, concat_axis=0, tiled=True
        )
        grad_value, grad_output = pl.pallas_call(
            last_kernel,
            out_shape=(jax.ShapeDtypeStruct((2, 512), F32),) * 2,
            in_specs=[VMEM],
            out_specs=(VMEM,) * 2,
            compiler_params=room(16),
            cost_estimate=cost(100000, 100000),
            name="last",
        )(line.reshape(512, 256))
        grad_output = jnp.transpose(grad_output)
    mixed, grad_tokens = pl.pallas_call(
        final_kernel,
        out_shape=(shape(256, 1024), shape(256, 1024)),
        in_specs=[HBM, VMEM] + [HBM] * 8,
        out_specs=(VMEM, VMEM),
        scratch_shapes=[
            buffer(256, 1024),
            buffer(2, 8, 128, 1024),
            pltpu.SemaphoreType.DMA((17,)),
        ],
        compiler_params=room(58),
        cost_estimate=cost(1200000000, 8000000),
        name="output_products",
    )(row_parts, returned, *weights)
    return (
        mixed.reshape(tokens.shape),
        grad_tokens.reshape(tokens.shape),
        grad_value,
        grad_output,
    )


def solution(mesh):
    fine = Mesh(mesh.devices.reshape(4, 2, 16, 2, 2), ("x", "yh", "z", "yl", "c"))
    dp, seq = ("x", "yh"), ("z", "yl", "c")
    return jax.shard_map(
        body,
        mesh=fine,
        in_specs=(
            P(dp, seq, None, None),
            P(dp, seq, None, None),
            P(None, seq, None, None),
            P(None, seq, None, None),
            P(dp, None),
            P(dp, None),
            P(dp, None),
            P(dp, None),
        ),
        out_specs=(
            P(dp, seq, None, None),
            P(dp, seq, None, None),
            P(dp + seq, None),
            P(None, dp + seq),
        ),
        check_vma=False,
    )
```

```python
import functools

import jax
import jax.numpy as jnp
from jax import lax
from jax.experimental import pallas as pl
from jax.experimental.pallas import tpu as pltpu
from jax.sharding import Mesh, PartitionSpec as P

HEAD_DIM = 64
ROWBLK = 128
COLBLK = 8
BF = jnp.bfloat16
F32 = jnp.float32
LAST = (((1,), (1,)), ((), ()))
FIRST = (((0,), (0,)), ((), ()))
MASKED = -1e30
VMEM = pl.BlockSpec(memory_space=pltpu.VMEM)
HBM = pl.BlockSpec(memory_space=pltpu.HBM)


def room(mebibytes):
    return pltpu.CompilerParams(vmem_limit_bytes=mebibytes * 1024 * 1024)


SWAP = [(0, 1), (1, 0)]
PAIR, PICK = 30000000000, 14000000000


def product(a, b, dims=(((1,), (0,)), ((), ()))):
    return lax.dot_general(a, b, dims, preferred_element_type=F32)


def eights(first, rows=256):
    row = lax.broadcasted_iota(jnp.int32, (2 * rows, rows), 0)
    col = lax.broadcasted_iota(jnp.int32, (2 * rows, rows), 1)
    inside = (row & 4) == (0 if first else 4)
    return ((col == (row >> 3) * 4 + (row & 3)) & inside).astype(F32).astype(BF)


def interleave(first, second, dims=(((1,), (0,)), ((), ()))):
    rows = first.shape[dims[0][1][0]]
    return (
        product(eights(True, rows), first, dims) + product(eights(False, rows), second, dims)
    ).astype(BF)


def separate(both):
    return tuple(product(eights(t), both, FIRST).astype(BF) for t in (True, False))


def start_copies(pairs, sems, first=0):
    copies = [
        pltpu.make_async_copy(source, target, sems.at[first + i])
        for i, (source, target) in enumerate(pairs)
    ]
    for copy in copies:
        copy.start()
    return copies


def wait_for(copies):
    for copy in copies:
        copy.wait()


def interleave_kernel(x_ref, ct_ref, sent_ref, x, ct, sent, sems):
    pieces = [(pl.ds(i * 64, 64), pl.ds(i * 128, 128)) for i in range(4)]
    loads, stores = [], []
    for rows, _ in pieces:
        loads += [(x_ref.at[rows], x.at[rows]), (ct_ref.at[rows], ct.at[rows])]
    copies = start_copies(loads, sems)
    for i, (rows, out) in enumerate(pieces):
        wait_for(copies[2 * i : 2 * i + 2])
        sent[out] = interleave(x[rows], ct[rows])
        stores += start_copies([(sent.at[out], sent_ref.at[out])], sems, 8 + i)
    wait_for(stores)


def pack_kernel(wq_ref, wk_ref, wv_ref, wo_ref, packed_ref, sems):
    core = lax.axis_index("c")
    here = pl.ds(pl.multiple_of(core * 256, 256), 256)
    pairs = []
    for i, ref in enumerate((wq_ref, wk_ref, wv_ref)):
        pairs.append((ref.at[:, here], packed_ref.at[:, pl.ds(i * 256, 256)]))
    for b in range(2):
        there = pl.ds(pl.multiple_of(core * 512 + b * 256, 256), 256)
        pairs.append((wo_ref.at[:, there], packed_ref.at[pl.ds(b * 64, 64), pl.ds(768, 256)]))
    wait_for(start_copies(pairs, sems))


def pair_kernel(packed_ref, flipped_ref, pair_ref):
    pair_ref[0] = packed_ref[...]
    pair_ref[1] = flipped_ref[...]


def attention(x_ref, ct_ref, weights, copies, kind, bias_ref):
    across = lax.axis_index("x")
    qkv = jnp.zeros((256, 768), F32)
    for step in range(4):
        wait_for(copies[2 * step : 2 * step + 2])
        source = (across + 4 - step) & 3
        left = x_ref[:, pl.ds(pl.multiple_of(source * 256, 256), 256)]
        qkv += product(left, weights[kind, pl.ds(source * 2, 2), :, 0:768].reshape(256, 768))
    qkv = qkv.astype(BF)
    q, k, v = qkv[:, :256], qkv[:, 256:512], qkv[:, 512:]
    wait_for(copies[8:])
    ct = ct_ref[...]
    do = jnp.zeros((256, 256), F32)
    for half in range(2):
        for b in range(2):
            block = weights[half, kind * 4 : kind * 4 + 4, b * 64 : (b + 1) * 64, 768:1024]
            start = half * 512 + b * 256
            do += product(ct[:, start : start + 256], block.reshape(256, 256), LAST)
    do = do.astype(BF)
    q = q * jnp.asarray(0.125, BF)
    qt, kt, vt, ot = q.T, (k * jnp.asarray(0.125, BF)).T, v.T, do.T
    lane = lax.broadcasted_iota(jnp.int32, (256, 256), 1) // HEAD_DIM
    zero = jnp.zeros_like(q)
    heads = range(4)
    s = [product(jnp.where(lane == h, q, zero), k, LAST) + bias_ref[h].astype(F32) for h in heads]
    e = [jnp.exp(a - jnp.max(a, axis=-1, keepdims=True)) for a in s]
    w = [a * (1.0 / jnp.sum(a, axis=-1, keepdims=True)) for a in e]
    p = [a.astype(BF) for a in w]
    dp = [product(jnp.where(lane == h, do, zero), v, LAST) for h in heads]
    ds = [(a * (b - jnp.sum(b * a, axis=-1, keepdims=True))).astype(BF) for a, b in zip(w, dp)]
    rows = [slice(h * HEAD_DIM, (h + 1) * HEAD_DIM) for h in heads]
    results = (
        [product(vt[rows[h]], p[h], LAST) for h in heads],
        [product(kt[rows[h]], ds[h], LAST) for h in heads],
        [product(qt[rows[h]], ds[h]) for h in heads],
        [product(ot[rows[h]], p[h]) for h in heads],
    )
    return tuple(jnp.concatenate(a, axis=0).astype(BF) for a in results)


def store_gradients(core, x, ct, outt, dvt, keep_ref, send_ref, done=lambda block: None):
    gradients = (product(dvt, x).astype(BF), product(outt, ct).astype(BF))
    new = lax.broadcasted_iota(jnp.int32, (128, 128), 0)
    old = lax.broadcasted_iota(jnp.int32, (128, 128), 1)
    source = ((new >> 1) & 31) * 4 + ((new >> 6) ^ core) * 2 + (new & 1)
    order = (old == source).astype(F32).astype(BF)
    for block in range(8):
        rows = slice(block * 64, (block + 1) * 64)
        for i, part in enumerate(gradients):
            moved = product(order, part[:, block * 128 : (block + 1) * 128], LAST).astype(BF)
            keep_ref[rows, i * 256 : (i + 1) * 256] = moved[:64]
            send_ref[rows, i * 256 : (i + 1) * 256] = moved[64:]
        done(block)


def weight_copies(refs, w_ref, sems, kinds):
    core, across, high = (lax.axis_index(name) for name in ("c", "x", "yh"))
    right = pl.ds(768, 256)
    pairs, sides = [], ([], [])
    for step in range(4):
        for flip in range(2):
            shard = ((across + 4 - step) & 3) * 2 + (high ^ flip)
            for side in range(2):
                ref = refs[4 * side + step].at[flip]
                half = core ^ side
                if kinds == 2:
                    pairs.append((ref, w_ref.at[half, shard]))
                else:
                    pairs.append((ref.at[:, right], w_ref.at[half, shard, :, right]))
                    left = pl.ds(0, 768)
                    sides[side].append((ref.at[:, left], w_ref.at[half, shard, :, left]))
    return pairs, sides


def kind_copies(kind, refs, w_ref, sems, first):
    pairs, sides = weight_copies(refs, w_ref, sems, 1)
    core = lax.axis_index("c")
    for side in range(2):

        @pl.when((core ^ side) == kind)
        def _(side=side):
            start_copies(sides[side], sems, first)

    waits = [
        pltpu.make_async_copy(source, target, sems.at[first + i])
        for i, (source, target) in enumerate(sides[0])
    ]
    return waits + start_copies(pairs, sems, first + 8)


def row_kernel(x_ref, ct_ref, bias_ref, *refs):
    weights, (parts_ref, keep_ref, send_ref, x_here, ct_here, bias, w_ref, sems) = refs[:8], refs[8:]
    copies = start_copies(((x_ref, x_here), (ct_ref, ct_here), (bias_ref, bias)), sems)
    more = kind_copies(0, weights, w_ref, sems, 3)
    wait_for(copies[:1])
    out, dq, dk, dv = attention(x_here, ct_here, w_ref, more + copies[1:], 0, bias)
    for i, part in enumerate((out, dq, dk, dv)):
        parts_ref[:, i * 256 : (i + 1) * 256] = part.T
    store_gradients(lax.axis_index("c"), x_here[...], ct_here[...], out, dv, keep_ref, send_ref)


def column_kernel(both_ref, bias_ref, *refs):
    weights, refs = refs[:8], refs[8:]
    parts_ref, keep_ref, send_ref, parts, keep, send, x, ct, bias, w_ref, sems = refs
    copies = kind_copies(1, weights, w_ref, sems, 1) + start_copies(((bias_ref, bias),), sems)
    x[...], ct[...] = separate(both_ref[...])
    out, dq, dk, dv = attention(x, ct, w_ref, copies, 1, bias)
    parts[:, 0:256] = interleave(out, dk, LAST)
    parts[:, 256:512] = interleave(dq, dv, LAST)
    stores = start_copies(((parts, parts_ref),), sems)


    def store(block):
        if block in (3, 7):
            rows = pl.ds((block - 3) * 64, 256)
            pairs = [(keep.at[rows], keep_ref.at[rows]), (send.at[rows], send_ref.at[rows])]
            stores.extend(start_copies(pairs, sems, block - 2))

    store_gradients(lax.axis_index("c"), x[...], ct[...], out, dv, keep, send, store)
    wait_for(stores)


def pick_kernel(row_keep, row_got, col_keep, col_got, *terms):
    across = lax.axis_index("x")
    for step, term in enumerate(terms):
        rows = pl.ds(pl.multiple_of(((across + step) & 3) * 128, 128), 128)
        for i, (keep, got) in enumerate(((row_keep, row_got), (col_keep, col_got))):
            total = keep[rows, :].astype(F32) + got[rows, :].astype(F32)
            term[:, i * 512 : (i + 1) * 512] = total.astype(BF)


def spread_kernel(*refs):
    given, keep_ref, send_ref, total = refs[:4], refs[4], refs[5], refs[6]
    total[...] = sum(ref[...].astype(F32) for ref in given).astype(BF)
    high = lax.axis_index("yh")
    keep_ref[...] = total[pl.ds(pl.multiple_of(high * 64, 64), 64), :]
    send_ref[...] = total[pl.ds(pl.multiple_of((high ^ 1) * 64, 64), 64), :]


def line_kernel(keep_ref, got_ref, out_ref):
    total = (keep_ref[...].astype(F32) + got_ref[...].astype(F32)).astype(BF)
    row = lax.broadcasted_iota(jnp.int32, (256, 64), 0)
    col = lax.broadcasted_iota(jnp.int32, (256, 64), 1)
    out = jnp.zeros((256, 256), F32)
    for b in range(4):
        here = (col == (row >> 3) * 2 + (row & 1)) & ((row & 6) == 2 * b)
        out += product(here.astype(F32).astype(BF), total[:, b * 256 : (b + 1) * 256])
    out_ref[...] = out.astype(BF)


def last_kernel(line_ref, value_ref, out_ref):
    total = jnp.sum(line_ref[...].astype(F32).reshape(32, 8, 256), axis=0)
    for kind in range(2):
        value_ref[:, kind * 256 : (kind + 1) * 256] = total[kind * 4 : kind * 4 + 2]
        out_ref[:, kind * 256 : (kind + 1) * 256] = total[kind * 4 + 2 : kind * 4 + 4]


def final_kernel(row_ref, col_ref, *refs):
    weights, (mixed_ref, gt_ref, row, w_ref, sems) = refs[:8], refs[8:]
    copies = start_copies(weight_copies(weights, w_ref, sems, 2)[0] + [(row_ref, row)], sems)
    first, second = separate(col_ref[...])
    wait_for(copies)
    sides = (
        (row[:, 0:256], row[:, 256:1024]),
        (first[:, 0:256], jnp.concatenate([first[:, 256:512], second], axis=1)),
    )
    for half in range(2):
        for b in range(2):
            total = jnp.zeros((256, 256), F32)
            for kind in range(2):
                block = w_ref[half, kind * 4 : kind * 4 + 4, b * 64 : (b + 1) * 64, 768:1024]
                total += product(sides[kind][0], block.reshape(256, 256))
            start = half * 512 + b * 256
            mixed_ref[:, start : start + 256] = total.astype(BF)
    total = jnp.zeros(gt_ref.shape, F32)
    for kind in range(2):
        total += product(sides[kind][1], w_ref[kind, :, :, 0:768].reshape(1024, 768), LAST)
    gt_ref[...] = total.astype(BF)


def shape(*dims):
    return jax.ShapeDtypeStruct(dims, BF)


def buffer(*dims):
    return pltpu.VMEM(dims, BF)


def cost(flops, moved):
    return pl.CostEstimate(flops=flops, bytes_accessed=moved, transcendentals=0)


def one_hot(index, size):
    return (index[:, None] == jnp.arange(size)[None, :]).astype(BF)


def biases(row_mask, column_mask):
    position = jnp.arange(256)
    seen = position[:, None] >= position[None, :]
    row_in = one_hot(position // ROWBLK, 2)
    row_blocks = jnp.einsum(
        "ia,hab,jb->hij", row_in, row_mask[:, 0].astype(BF), row_in, preferred_element_type=BF
    )
    same = (position[:, None] % 4) == (position[None, :] % 4)
    col_left = one_hot((position % 4) * 8 + position // (4 * COLBLK), 32)
    col_right = one_hot(position // (4 * COLBLK), 8)
    col_blocks = jnp.einsum(
        "ia,hab,jb->hij",
        col_left,
        column_mask.reshape(4, 32, 8).astype(BF),
        col_right,
        preferred_element_type=BF,
    )
    row_bias = jnp.where((row_blocks > 0.5) & seen, 0.0, MASKED).astype(BF)
    col_bias = jnp.where((col_blocks > 0.5) & seen & same, 0.0, MASKED).astype(BF)
    return row_bias, col_bias


def body(tokens, cotangent, row_mask, column_mask, w_query, w_key, w_value, w_out):
    flat = tokens.reshape(256, 1024)
    cot_flat = cotangent.reshape(256, 1024)
    seq = ("z", "yl", "c")

    sent = pl.pallas_call(
        interleave_kernel,
        out_shape=shape(512, 1024),
        in_specs=[HBM] * 2,
        out_specs=HBM,
        scratch_shapes=[
            buffer(256, 1024),
            buffer(256, 1024),
            buffer(512, 1024),
            pltpu.SemaphoreType.DMA((12,)),
        ],
        compiler_params=room(60),
        cost_estimate=cost(540000000, 2000000),
        name="interleave",
    )(flat, cot_flat)
    packed = pl.pallas_call(
        pack_kernel,
        out_shape=shape(128, 1024),
        in_specs=[HBM] * 4,
        out_specs=VMEM,
        scratch_shapes=[pltpu.SemaphoreType.DMA((5,))],
        compiler_params=room(60),
        cost_estimate=cost(1000000000, 2000000),
        name="pack",
    )(w_query, w_key, w_value, w_out)
    with jax.named_scope("to_columns"):
        both = lax.all_to_all(
            sent.reshape(64, 8, 1024), seq, split_axis=0, concat_axis=0, tiled=True
        ).reshape(512, 1024)
    with jax.named_scope("masks"):
        row_bias, col_bias = biases(row_mask, column_mask)
    with jax.named_scope("weights"):
        flipped = lax.ppermute(packed, ("yh", "yl"), [(y, 3 - y) for y in range(4)])
        pair = pl.pallas_call(
            pair_kernel,
            out_shape=shape(2, 128, 1024),
            in_specs=[VMEM] * 2,
            out_specs=VMEM,
            compiler_params=room(16),
            cost_estimate=cost(PAIR, 1000000),
            name="pair",
        )(packed, flipped)
        weights = [pair] + [
            lax.ppermute(pair, "x", [(x, (x + step) % 4) for x in range(4)]) for step in (1, 2, 3)
        ]
        weights[3], row_bias, col_bias = lax.optimization_barrier((weights[3], row_bias, col_bias))
        weights += [lax.ppermute(part, "c", SWAP) for part in weights]
    row_parts, row_keep, row_send = pl.pallas_call(
        row_kernel,
        out_shape=(shape(256, 1024), shape(512, 512), shape(512, 512)),
        in_specs=[HBM] * 11,
        out_specs=(VMEM,) * 3,
        scratch_shapes=[
            buffer(256, 1024),
            buffer(256, 1024),
            buffer(4, 256, 256),
            buffer(2, 8, 128, 1024),
            pltpu.SemaphoreType.DMA((27,)),
        ],
        compiler_params=room(58),
        cost_estimate=cost(1400000000, 12000000),
        name="row_heads",
    )(flat, cot_flat, row_bias, *weights)
    row_got = lax.ppermute(row_send, "c", SWAP)
    both, row_keep = lax.optimization_barrier((both, row_keep))
    col_parts, col_keep, col_send = pl.pallas_call(
        column_kernel,
        out_shape=(shape(512, 512),) * 3,
        in_specs=[VMEM] + [HBM] * 9,
        out_specs=(HBM,) * 3,
        scratch_shapes=[
            buffer(512, 512),
            buffer(512, 512),
            buffer(512, 512),
            buffer(256, 1024),
            buffer(256, 1024),
            buffer(4, 256, 256),
            buffer(2, 8, 128, 1024),
            pltpu.SemaphoreType.DMA((25,)),
        ],
        compiler_params=room(58),
        cost_estimate=cost(1900000000, 8000000),
        name="column_heads",
    )(both, col_bias, *weights)
    col_got = lax.ppermute(col_send, "c", SWAP)
    with jax.named_scope("from_columns"):
        returned = lax.all_to_all(
            col_parts.reshape(64, 8, 512), seq, split_axis=0, concat_axis=0, tiled=True
        ).reshape(512, 512)

    with jax.named_scope("gradient_sums"):
        terms = pl.pallas_call(
            pick_kernel,
            out_shape=(shape(128, 1024),) * 4,
            in_specs=[VMEM] * 4,
            out_specs=(VMEM,) * 4,
            compiler_params=room(16),
            cost_estimate=cost(PICK, 3000000),
            name="pick",
        )(row_keep, row_got, col_keep, col_got)
        moved = [
            lax.ppermute(terms[step], "x", [(x, (x + step) % 4) for x in range(4)])
            for step in (2, 1, 3)
        ]
        line_keep, line_send = pl.pallas_call(
            spread_kernel,
            out_shape=(shape(64, 1024),) * 2,
            in_specs=[VMEM] * 4,
            out_specs=(VMEM,) * 2,
            scratch_shapes=[buffer(128, 1024)],
            compiler_params=room(16),
            cost_estimate=cost(10000000, 1000000),
            name="spread",
        )(terms[0], *moved)
        line_got = lax.ppermute(line_send, ("yh", "yl"), [(y, 3 - y) for y in range(4)])
        line = pl.pallas_call(
            line_kernel,
            out_shape=shape(256, 256),
            in_specs=[VMEM] * 2,
            out_specs=VMEM,
            compiler_params=room(16),
            cost_estimate=cost(10000000, 300000),
            name="line",
        )(line_keep, line_got)
        line, returned = lax.optimization_barrier((line, returned))
        line = lax.all_to_all(
            line.reshape(32, 8, 256), ("z", "yl"), split_axis=0, concat_axis=0, tiled=True
        )
        grad_value, grad_output = pl.pallas_call(
            last_kernel,
            out_shape=(jax.ShapeDtypeStruct((2, 512), F32),) * 2,
            in_specs=[VMEM],
            out_specs=(VMEM,) * 2,
            compiler_params=room(16),
            cost_estimate=cost(100000, 100000),
            name="last",
        )(line.reshape(256, 256))
        grad_output = jnp.transpose(grad_output)
    mixed, grad_tokens = pl.pallas_call(
        final_kernel,
        out_shape=(shape(256, 1024), shape(256, 1024)),
        in_specs=[HBM, VMEM] + [HBM] * 8,
        out_specs=(VMEM, VMEM),
        scratch_shapes=[
            buffer(256, 1024),
            buffer(2, 8, 128, 1024),
            pltpu.SemaphoreType.DMA((17,)),
        ],
        compiler_params=room(58),
        cost_estimate=cost(1200000000, 8000000),
        name="output_products",
    )(row_parts, returned, *weights)
    return (
        mixed.reshape(tokens.shape),
        grad_tokens.reshape(tokens.shape),
        grad_value,
        grad_output,
    )


def solution(mesh):
    fine = Mesh(mesh.devices.reshape(4, 2, 16, 2, 2), ("x", "yh", "z", "yl", "c"))
    dp, seq = ("x", "yh"), ("z", "yl", "c")
    return jax.shard_map(
        body,
        mesh=fine,
        in_specs=(
            P(dp, seq, None, None),
            P(dp, seq, None, None),
            P(None, seq, None, None),
            P(None, seq, None, None),
            P(dp, None),
            P(dp, None),
            P(dp, None),
            P(dp, None),
        ),
        out_specs=(
            P(dp, seq, None, None),
            P(dp, seq, None, None),
            P(dp + seq, None),
            P(None, dp + seq),
        ),
        check_vma=False,
    )
```

```python
import functools

import jax
import jax.numpy as jnp
from jax import lax
from jax.experimental import pallas as pl
from jax.experimental.pallas import tpu as pltpu
from jax.sharding import Mesh, PartitionSpec as P

HEAD_DIM = 64
ROWBLK = 128
COLBLK = 8
BF = jnp.bfloat16
F32 = jnp.float32
LAST = (((1,), (1,)), ((), ()))
FIRST = (((0,), (0,)), ((), ()))
MASKED = -1e30
VMEM = pl.BlockSpec(memory_space=pltpu.VMEM)
HBM = pl.BlockSpec(memory_space=pltpu.HBM)


def room(mebibytes):
    return pltpu.CompilerParams(vmem_limit_bytes=mebibytes * 1024 * 1024)


SWAP = [(0, 1), (1, 0)]
PAIR, PICK = 30000000000, 14000000000


def product(a, b, dims=(((1,), (0,)), ((), ()))):
    return lax.dot_general(a, b, dims, preferred_element_type=F32)


def eights(first, rows=256):
    row = lax.broadcasted_iota(jnp.int32, (2 * rows, rows), 0)
    col = lax.broadcasted_iota(jnp.int32, (2 * rows, rows), 1)
    row = row ^ (256 if rows == 256 else 0)
    inside = (row & 4) == (0 if first else 4)
    return ((col == (row >> 3) * 4 + (row & 3)) & inside).astype(F32).astype(BF)


def interleave(first, second, dims=(((1,), (0,)), ((), ()))):
    rows = first.shape[dims[0][1][0]]
    return (
        product(eights(True, rows), first, dims) + product(eights(False, rows), second, dims)
    ).astype(BF)


def separate(both):
    return tuple(product(eights(t), both, FIRST).astype(BF) for t in (True, False))


def start_copies(pairs, sems, first=0):
    copies = [
        pltpu.make_async_copy(source, target, sems.at[first + i])
        for i, (source, target) in enumerate(pairs)
    ]
    for copy in copies:
        copy.start()
    return copies


def wait_for(copies):
    for copy in copies:
        copy.wait()


def interleave_kernel(x_ref, ct_ref, sent_ref, sent, sems):
    stores = []
    for i in range(4):
        rows, out = pl.ds(i * 64, 64), pl.ds((i ^ 2) * 128, 128)
        sent[out] = interleave(x_ref[rows], ct_ref[rows])
        stores += start_copies([(sent.at[out], sent_ref.at[out])], sems, i)
    wait_for(stores)


def pack_kernel(wq_ref, wk_ref, wv_ref, wo_ref, packed_ref, sems):
    core = lax.axis_index("c")
    here = pl.ds(pl.multiple_of(core * 256, 256), 256)
    pairs = []
    for i, ref in enumerate((wq_ref, wk_ref, wv_ref)):
        pairs.append((ref.at[:, here], packed_ref.at[:, pl.ds(i * 256, 256)]))
    for b in range(2):
        there = pl.ds(pl.multiple_of(core * 512 + b * 256, 256), 256)
        pairs.append((wo_ref.at[:, there], packed_ref.at[pl.ds(b * 64, 64), pl.ds(768, 256)]))
    wait_for(start_copies(pairs, sems))


def pair_kernel(packed_ref, flipped_ref, pair_ref):
    pair_ref[0] = packed_ref[...]
    pair_ref[1] = flipped_ref[...]


def attention(x_ref, ct_ref, weights, copies, kind, bias_ref):
    across = lax.axis_index("x")
    qkv = jnp.zeros((256, 768), F32)
    for step in range(4):
        wait_for(copies[2 * step : 2 * step + 2])
        source = (across + 4 - step) & 3
        left = x_ref[:, pl.ds(pl.multiple_of(source * 256, 256), 256)]
        qkv += product(left, weights[kind, pl.ds(source * 2, 2), :, 0:768].reshape(256, 768))
    qkv = qkv.astype(BF)
    q, k, v = qkv[:, :256], qkv[:, 256:512], qkv[:, 512:]
    wait_for(copies[8:])
    ct = ct_ref[...]
    do = jnp.zeros((256, 256), F32)
    for half in range(2):
        for b in range(2):
            block = weights[half, kind * 4 : kind * 4 + 4, b * 64 : (b + 1) * 64, 768:1024]
            start = half * 512 + b * 256
            do += product(ct[:, start : start + 256], block.reshape(256, 256), LAST)
    do = do.astype(BF)
    q = q * jnp.asarray(0.125, BF)
    qt, kt, vt, ot = q.T, (k * jnp.asarray(0.125, BF)).T, v.T, do.T
    lane = lax.broadcasted_iota(jnp.int32, (256, 256), 1) // HEAD_DIM
    zero = jnp.zeros_like(q)
    heads = range(4)
    s = [product(jnp.where(lane == h, q, zero), k, LAST) + bias_ref[h].astype(F32) for h in heads]
    e = [jnp.exp(a - jnp.max(a, axis=-1, keepdims=True)) for a in s]
    w = [a * (1.0 / jnp.sum(a, axis=-1, keepdims=True)) for a in e]
    p = [a.astype(BF) for a in w]
    dp = [product(jnp.where(lane == h, do, zero), v, LAST) for h in heads]
    ds = [(a * (b - jnp.sum(b * a, axis=-1, keepdims=True))).astype(BF) for a, b in zip(w, dp)]
    rows = [slice(h * HEAD_DIM, (h + 1) * HEAD_DIM) for h in heads]
    results = (
        [product(vt[rows[h]], p[h], LAST) for h in heads],
        [product(kt[rows[h]], ds[h], LAST) for h in heads],
        [product(qt[rows[h]], ds[h]) for h in heads],
        [product(ot[rows[h]], p[h]) for h in heads],
    )
    return tuple(jnp.concatenate(a, axis=0).astype(BF) for a in results)


def store_gradients(core, x, ct, outt, dvt, keep_ref, send_ref, done=lambda block: None):
    gradients = (product(dvt, x).astype(BF), product(outt, ct).astype(BF))
    new = lax.broadcasted_iota(jnp.int32, (128, 128), 0)
    old = lax.broadcasted_iota(jnp.int32, (128, 128), 1)
    source = ((new >> 1) & 31) * 4 + ((new >> 6) ^ core) * 2 + (new & 1)
    order = (old == source).astype(F32).astype(BF)
    for block in range(8):
        rows = slice(block * 64, (block + 1) * 64)
        for i, part in enumerate(gradients):
            moved = product(order, part[:, block * 128 : (block + 1) * 128], LAST).astype(BF)
            keep_ref[rows, i * 256 : (i + 1) * 256] = moved[:64]
            send_ref[rows, i * 256 : (i + 1) * 256] = moved[64:]
        done(block)


def weight_copies(refs, w_ref, sems, kinds):
    core, across, high = (lax.axis_index(name) for name in ("c", "x", "yh"))
    right = pl.ds(768, 256)
    pairs, sides = [], ([], [])
    for step in range(4):
        for flip in range(2):
            shard = ((across + 4 - step) & 3) * 2 + (high ^ flip)
            for side in range(2):
                ref = refs[4 * side + step].at[flip]
                half = core ^ side
                if kinds == 2:
                    pairs.append((ref, w_ref.at[half, shard]))
                else:
                    pairs.append((ref.at[:, right], w_ref.at[half, shard, :, right]))
                    left = pl.ds(0, 768)
                    sides[side].append((ref.at[:, left], w_ref.at[half, shard, :, left]))
    return pairs, sides


def kind_copies(kind, refs, w_ref, sems, first):
    pairs, sides = weight_copies(refs, w_ref, sems, 1)
    core = lax.axis_index("c")
    for side in range(2):

        @pl.when((core ^ side) == kind)
        def _(side=side):
            start_copies(sides[side], sems, first)

    waits = [
        pltpu.make_async_copy(source, target, sems.at[first + i])
        for i, (source, target) in enumerate(sides[0])
    ]
    return waits + start_copies(pairs, sems, first + 8)


def row_kernel(x_ref, ct_ref, bias_ref, *refs):
    weights, (parts_ref, keep_ref, send_ref, x_here, ct_here, bias, w_ref, sems) = refs[:8], refs[8:]
    copies = start_copies(((x_ref, x_here), (ct_ref, ct_here), (bias_ref, bias)), sems)
    more = kind_copies(0, weights, w_ref, sems, 3)
    wait_for(copies[:1])
    out, dq, dk, dv = attention(x_here, ct_here, w_ref, more + copies[1:], 0, bias)
    for i, part in enumerate((out, dq, dk, dv)):
        parts_ref[:, i * 256 : (i + 1) * 256] = part.T
    store_gradients(lax.axis_index("c"), x_here[...], ct_here[...], out, dv, keep_ref, send_ref)


def column_kernel(both_ref, bias_ref, *refs):
    weights, refs = refs[:8], refs[8:]
    parts_ref, keep_ref, send_ref, parts, keep, send, x, ct, bias, w_ref, sems = refs
    copies = kind_copies(1, weights, w_ref, sems, 1) + start_copies(((bias_ref, bias),), sems)
    x[...], ct[...] = separate(both_ref[...])
    out, dq, dk, dv = attention(x, ct, w_ref, copies, 1, bias)
    parts[:, 0:256] = interleave(out, dk, LAST)
    parts[:, 256:512] = interleave(dq, dv, LAST)
    stores = start_copies(((parts, parts_ref),), sems)


    def store(block):
        if block in (3, 7):
            rows = pl.ds((block - 3) * 64, 256)
            pairs = [(keep.at[rows], keep_ref.at[rows]), (send.at[rows], send_ref.at[rows])]
            stores.extend(start_copies(pairs, sems, block - 2))

    store_gradients(lax.axis_index("c"), x[...], ct[...], out, dv, keep, send, store)
    wait_for(stores)


def pick_kernel(row_keep, row_got, col_keep, col_got, *terms):
    across = lax.axis_index("x")
    for step, term in enumerate(terms):
        rows = pl.ds(pl.multiple_of(((across + step) & 3) * 128, 128), 128)
        for i, (keep, got) in enumerate(((row_keep, row_got), (col_keep, col_got))):
            total = keep[rows, :].astype(F32) + got[rows, :].astype(F32)
            term[:, i * 512 : (i + 1) * 512] = total.astype(BF)


def spread_kernel(*refs):
    given, keep_ref, send_ref, total = refs[:4], refs[4], refs[5], refs[6]
    total[...] = sum(ref[...].astype(F32) for ref in given).astype(BF)
    high = lax.axis_index("yh")
    keep_ref[...] = total[pl.ds(pl.multiple_of(high * 64, 64), 64), :]
    send_ref[...] = total[pl.ds(pl.multiple_of((high ^ 1) * 64, 64), 64), :]


def line_kernel(keep_ref, got_ref, out_ref):
    total = (keep_ref[...].astype(F32) + got_ref[...].astype(F32)).astype(BF)
    row = lax.broadcasted_iota(jnp.int32, (256, 64), 0)
    col = lax.broadcasted_iota(jnp.int32, (256, 64), 1)
    out = jnp.zeros((256, 256), F32)
    for b in range(4):
        here = (col == ((row >> 3) ^ 16) * 2 + (row & 1)) & ((row & 6) == 2 * b)
        out += product(here.astype(F32).astype(BF), total[:, b * 256 : (b + 1) * 256])
    out_ref[...] = out.astype(BF)


def last_kernel(line_ref, value_ref, out_ref):
    total = jnp.sum(line_ref[...].astype(F32).reshape(32, 8, 256), axis=0)
    for kind in range(2):
        value_ref[:, kind * 256 : (kind + 1) * 256] = total[kind * 4 : kind * 4 + 2]
        out_ref[:, kind * 256 : (kind + 1) * 256] = total[kind * 4 + 2 : kind * 4 + 4]


def final_kernel(row_ref, col_ref, *refs):
    weights, (mixed_ref, gt_ref, row, w_ref, sems) = refs[:8], refs[8:]
    copies = start_copies(weight_copies(weights, w_ref, sems, 2)[0] + [(row_ref, row)], sems)
    first, second = separate(col_ref[...])
    wait_for(copies)
    sides = (
        (row[:, 0:256], row[:, 256:1024]),
        (first[:, 0:256], jnp.concatenate([first[:, 256:512], second], axis=1)),
    )
    for half in range(2):
        for b in range(2):
            total = jnp.zeros((256, 256), F32)
            for kind in range(2):
                block = w_ref[half, kind * 4 : kind * 4 + 4, b * 64 : (b + 1) * 64, 768:1024]
                total += product(sides[kind][0], block.reshape(256, 256))
            start = half * 512 + b * 256
            mixed_ref[:, start : start + 256] = total.astype(BF)
    total = jnp.zeros(gt_ref.shape, F32)
    for kind in range(2):
        total += product(sides[kind][1], w_ref[kind, :, :, 0:768].reshape(1024, 768), LAST)
    gt_ref[...] = total.astype(BF)


def shape(*dims):
    return jax.ShapeDtypeStruct(dims, BF)


def buffer(*dims):
    return pltpu.VMEM(dims, BF)


def cost(flops, moved):
    return pl.CostEstimate(flops=flops, bytes_accessed=moved, transcendentals=0)


def one_hot(index, size):
    return (index[:, None] == jnp.arange(size)[None, :]).astype(BF)


def biases(row_mask, column_mask):
    position = jnp.arange(256)
    seen = position[:, None] >= position[None, :]
    row_in = one_hot(position // ROWBLK, 2)
    row_blocks = jnp.einsum(
        "ia,hab,jb->hij", row_in, row_mask[:, 0].astype(BF), row_in, preferred_element_type=BF
    )
    same = (position[:, None] % 4) == (position[None, :] % 4)
    col_left = one_hot((position % 4) * 8 + position // (4 * COLBLK), 32)
    col_right = one_hot(position // (4 * COLBLK), 8)
    col_blocks = jnp.einsum(
        "ia,hab,jb->hij",
        col_left,
        column_mask.reshape(4, 32, 8).astype(BF),
        col_right,
        preferred_element_type=BF,
    )
    row_bias = jnp.where((row_blocks > 0.5) & seen, 0.0, MASKED).astype(BF)
    col_bias = jnp.where((col_blocks > 0.5) & seen & same, 0.0, MASKED).astype(BF)
    return row_bias, col_bias


def body(tokens, cotangent, row_mask, column_mask, w_query, w_key, w_value, w_out):
    flat = tokens.reshape(256, 1024)
    cot_flat = cotangent.reshape(256, 1024)
    seq = ("z", "yl", "c")

    sent = pl.pallas_call(
        interleave_kernel,
        out_shape=shape(512, 1024),
        in_specs=[VMEM] * 2,
        out_specs=HBM,
        scratch_shapes=[buffer(512, 1024), pltpu.SemaphoreType.DMA((4,))],
        compiler_params=room(16),
        cost_estimate=cost(540000000, 2000000),
        name="interleave",
    )(flat, cot_flat)
    packed = pl.pallas_call(
        pack_kernel,
        out_shape=shape(128, 1024),
        in_specs=[HBM] * 4,
        out_specs=VMEM,
        scratch_shapes=[pltpu.SemaphoreType.DMA((5,))],
        compiler_params=room(60),
        cost_estimate=cost(1000000000, 2000000),
        name="pack",
    )(w_query, w_key, w_value, w_out)
    with jax.named_scope("to_columns"):
        both = lax.all_to_all(
            sent.reshape(64, 8, 1024), seq, split_axis=0, concat_axis=0, tiled=True, axis_index_groups=[[p ^ 32 for p in range(64)]]
        ).reshape(512, 1024)
    with jax.named_scope("masks"):
        row_bias, col_bias = biases(row_mask, column_mask)
    with jax.named_scope("weights"):
        flipped = lax.ppermute(packed, ("yh", "yl"), [(y, 3 - y) for y in range(4)])
        pair = pl.pallas_call(
            pair_kernel,
            out_shape=shape(2, 128, 1024),
            in_specs=[VMEM] * 2,
            out_specs=VMEM,
            compiler_params=room(16),
            cost_estimate=cost(PAIR, 1000000),
            name="pair",
        )(packed, flipped)
        weights = [pair] + [
            lax.ppermute(pair, "x", [(x, (x + step) % 4) for x in range(4)]) for step in (1, 2, 3)
        ]
        weights[3], row_bias, col_bias = lax.optimization_barrier((weights[3], row_bias, col_bias))
        weights += [lax.ppermute(part, "c", SWAP) for part in weights]
    row_parts, row_keep, row_send = pl.pallas_call(
        row_kernel,
        out_shape=(shape(256, 1024), shape(512, 512), shape(512, 512)),
        in_specs=[HBM] * 11,
        out_specs=(VMEM,) * 3,
        scratch_shapes=[
            buffer(256, 1024),
            buffer(256, 1024),
            buffer(4, 256, 256),
            buffer(2, 8, 128, 1024),
            pltpu.SemaphoreType.DMA((27,)),
        ],
        compiler_params=room(58),
        cost_estimate=cost(1400000000, 12000000),
        name="row_heads",
    )(flat, cot_flat, row_bias, *weights)
    row_got = lax.ppermute(row_send, "c", SWAP)
    both, row_keep = lax.optimization_barrier((both, row_keep))
    col_parts, col_keep, col_send = pl.pallas_call(
        column_kernel,
        out_shape=(shape(512, 512),) * 3,
        in_specs=[VMEM] + [HBM] * 9,
        out_specs=(HBM,) * 3,
        scratch_shapes=[
            buffer(512, 512),
            buffer(512, 512),
            buffer(512, 512),
            buffer(256, 1024),
            buffer(256, 1024),
            buffer(4, 256, 256),
            buffer(2, 8, 128, 1024),
            pltpu.SemaphoreType.DMA((25,)),
        ],
        compiler_params=room(58),
        cost_estimate=cost(1900000000, 8000000),
        name="column_heads",
    )(both, col_bias, *weights)
    col_got = lax.ppermute(col_send, "c", SWAP)
    with jax.named_scope("from_columns"):
        returned = lax.all_to_all(
            col_parts.reshape(64, 8, 512), seq, split_axis=0, concat_axis=0, tiled=True, axis_index_groups=[[p ^ 32 for p in range(64)]]
        ).reshape(512, 512)

    with jax.named_scope("gradient_sums"):
        terms = pl.pallas_call(
            pick_kernel,
            out_shape=(shape(128, 1024),) * 4,
            in_specs=[VMEM] * 4,
            out_specs=(VMEM,) * 4,
            compiler_params=room(16),
            cost_estimate=cost(PICK, 3000000),
            name="pick",
        )(row_keep, row_got, col_keep, col_got)
        moved = [
            lax.ppermute(terms[step], "x", [(x, (x + step) % 4) for x in range(4)])
            for step in (2, 1, 3)
        ]
        line_keep, line_send = pl.pallas_call(
            spread_kernel,
            out_shape=(shape(64, 1024),) * 2,
            in_specs=[VMEM] * 4,
            out_specs=(VMEM,) * 2,
            scratch_shapes=[buffer(128, 1024)],
            compiler_params=room(16),
            cost_estimate=cost(10000000, 1000000),
            name="spread",
        )(terms[0], *moved)
        line_got = lax.ppermute(line_send, ("yh", "yl"), [(y, 3 - y) for y in range(4)])
        line = pl.pallas_call(
            line_kernel,
            out_shape=shape(256, 256),
            in_specs=[VMEM] * 2,
            out_specs=VMEM,
            compiler_params=room(16),
            cost_estimate=cost(10000000, 300000),
            name="line",
        )(line_keep, line_got)
        line, returned = lax.optimization_barrier((line, returned))
        line = lax.all_to_all(
            line.reshape(32, 8, 256), ("z", "yl"), split_axis=0, concat_axis=0, tiled=True, axis_index_groups=[[p ^ 16 for p in range(32)]]
        )
        grad_value, grad_output = pl.pallas_call(
            last_kernel,
            out_shape=(jax.ShapeDtypeStruct((2, 512), F32),) * 2,
            in_specs=[VMEM],
            out_specs=(VMEM,) * 2,
            compiler_params=room(16),
            cost_estimate=cost(100000, 100000),
            name="last",
        )(line.reshape(256, 256))
        grad_output = jnp.transpose(grad_output)
    mixed, grad_tokens = pl.pallas_call(
        final_kernel,
        out_shape=(shape(256, 1024), shape(256, 1024)),
        in_specs=[HBM, VMEM] + [HBM] * 8,
        out_specs=(VMEM, VMEM),
        scratch_shapes=[
            buffer(256, 1024),
            buffer(2, 8, 128, 1024),
            pltpu.SemaphoreType.DMA((17,)),
        ],
        compiler_params=room(58),
        cost_estimate=cost(1200000000, 8000000),
        name="output_products",
    )(row_parts, returned, *weights)
    return (
        mixed.reshape(tokens.shape),
        grad_tokens.reshape(tokens.shape),
        grad_value,
        grad_output,
    )


def solution(mesh):
    fine = Mesh(mesh.devices.reshape(4, 2, 16, 2, 2), ("x", "yh", "z", "yl", "c"))
    dp, seq = ("x", "yh"), ("z", "yl", "c")
    return jax.shard_map(
        body,
        mesh=fine,
        in_specs=(
            P(dp, seq, None, None),
            P(dp, seq, None, None),
            P(None, seq, None, None),
            P(None, seq, None, None),
            P(dp, None),
            P(dp, None),
            P(dp, None),
            P(dp, None),
        ),
        out_specs=(
            P(dp, seq, None, None),
            P(dp, seq, None, None),
            P(dp + seq, None),
            P(None, dp + seq),
        ),
        check_vma=False,
    )
```

```python
import functools

import jax
import jax.numpy as jnp
from jax import lax
from jax.experimental import pallas as pl
from jax.experimental.pallas import tpu as pltpu
from jax.sharding import Mesh, PartitionSpec as P

HEAD_DIM = 64
ROWBLK = 128
COLBLK = 8
BF = jnp.bfloat16
F32 = jnp.float32
LAST = (((1,), (1,)), ((), ()))
FIRST = (((0,), (0,)), ((), ()))
MASKED = -1e30
VMEM = pl.BlockSpec(memory_space=pltpu.VMEM)
HBM = pl.BlockSpec(memory_space=pltpu.HBM)


def room(mebibytes):
    return pltpu.CompilerParams(vmem_limit_bytes=mebibytes * 1024 * 1024)


SWAP = [(0, 1), (1, 0)]
BEGIN, BEGIN_LAST = 10, 9
PAIR, PICK = 30000000000, 14000000000


def product(a, b, dims=(((1,), (0,)), ((), ()))):
    return lax.dot_general(a, b, dims, preferred_element_type=F32)


def member(place, rest, begin):
    return (place + begin * rest) & (16 * rest - 1)


def groups(rest, begin):
    return [[member(place, rest, begin) for place in range(16 * rest)]]


def eights(first, start=0, rows=512):
    row = lax.broadcasted_iota(jnp.int32, (rows, 256), 0) + start
    col = lax.broadcasted_iota(jnp.int32, (rows, 256), 1)
    inside = (row & 4) == (0 if first else 4)
    return ((col == member(row >> 3, 4, BEGIN) * 4 + (row & 3)) & inside).astype(F32).astype(BF)


def interleave(first, second, dims=(((1,), (0,)), ((), ())), start=0, rows=512):
    return (
        product(eights(True, start, rows), first, dims)
        + product(eights(False, start, rows), second, dims)
    ).astype(BF)


def separate(both):
    return tuple(product(eights(t), both, FIRST).astype(BF) for t in (True, False))


def start_copies(pairs, sems, first=0):
    copies = [
        pltpu.make_async_copy(source, target, sems.at[first + i])
        for i, (source, target) in enumerate(pairs)
    ]
    for copy in copies:
        copy.start()
    return copies


def wait_for(copies):
    for copy in copies:
        copy.wait()


def interleave_kernel(x_ref, ct_ref, sent_ref, sent, sems):
    stores = []
    for i in range(4):
        out = pl.ds(i * 128, 128)
        sent[out] = interleave(x_ref[...], ct_ref[...], start=i * 128, rows=128)
        stores += start_copies([(sent.at[out], sent_ref.at[out])], sems, i)
    wait_for(stores)


def pack_kernel(wq_ref, wk_ref, wv_ref, wo_ref, packed_ref, sems):
    core = lax.axis_index("c")
    here = pl.ds(pl.multiple_of(core * 256, 256), 256)
    pairs = []
    for i, ref in enumerate((wq_ref, wk_ref, wv_ref)):
        pairs.append((ref.at[:, here], packed_ref.at[:, pl.ds(i * 256, 256)]))
    for b in range(2):
        there = pl.ds(pl.multiple_of(core * 512 + b * 256, 256), 256)
        pairs.append((wo_ref.at[:, there], packed_ref.at[pl.ds(b * 64, 64), pl.ds(768, 256)]))
    wait_for(start_copies(pairs, sems))


def pair_kernel(packed_ref, flipped_ref, pair_ref):
    pair_ref[0] = packed_ref[...]
    pair_ref[1] = flipped_ref[...]


def attention(x_ref, ct_ref, weights, copies, kind, bias_ref):
    across = lax.axis_index("x")
    qkv = jnp.zeros((256, 768), F32)
    for step in range(4):
        wait_for(copies[2 * step : 2 * step + 2])
        source = (across + 4 - step) & 3
        left = x_ref[:, pl.ds(pl.multiple_of(source * 256, 256), 256)]
        qkv += product(left, weights[kind, pl.ds(source * 2, 2), :, 0:768].reshape(256, 768))
    qkv = qkv.astype(BF)
    q, k, v = qkv[:, :256], qkv[:, 256:512], qkv[:, 512:]
    wait_for(copies[8:])
    ct = ct_ref[...]
    do = jnp.zeros((256, 256), F32)
    for half in range(2):
        for b in range(2):
            block = weights[half, kind * 4 : kind * 4 + 4, b * 64 : (b + 1) * 64, 768:1024]
            start = half * 512 + b * 256
            do += product(ct[:, start : start + 256], block.reshape(256, 256), LAST)
    do = do.astype(BF)
    q = q * jnp.asarray(0.125, BF)
    qt, kt, vt, ot = q.T, (k * jnp.asarray(0.125, BF)).T, v.T, do.T
    lane = lax.broadcasted_iota(jnp.int32, (256, 256), 1) // HEAD_DIM
    zero = jnp.zeros_like(q)
    heads = range(4)
    s = [product(jnp.where(lane == h, q, zero), k, LAST) + bias_ref[h].astype(F32) for h in heads]
    e = [jnp.exp(a - jnp.max(a, axis=-1, keepdims=True)) for a in s]
    w = [a * (1.0 / jnp.sum(a, axis=-1, keepdims=True)) for a in e]
    p = [a.astype(BF) for a in w]
    dp = [product(jnp.where(lane == h, do, zero), v, LAST) for h in heads]
    ds = [(a * (b - jnp.sum(b * a, axis=-1, keepdims=True))).astype(BF) for a, b in zip(w, dp)]
    rows = [slice(h * HEAD_DIM, (h + 1) * HEAD_DIM) for h in heads]
    results = (
        [product(vt[rows[h]], p[h], LAST) for h in heads],
        [product(kt[rows[h]], ds[h], LAST) for h in heads],
        [product(qt[rows[h]], ds[h]) for h in heads],
        [product(ot[rows[h]], p[h]) for h in heads],
    )
    return tuple(jnp.concatenate(a, axis=0).astype(BF) for a in results)


def store_gradients(core, x, ct, outt, dvt, keep_ref, send_ref, done=lambda block: None):
    gradients = (product(dvt, x).astype(BF), product(outt, ct).astype(BF))
    new = lax.broadcasted_iota(jnp.int32, (128, 128), 0)
    old = lax.broadcasted_iota(jnp.int32, (128, 128), 1)
    source = ((new >> 1) & 31) * 4 + ((new >> 6) ^ core) * 2 + (new & 1)
    order = (old == source).astype(F32).astype(BF)
    for block in range(8):
        rows = slice(block * 64, (block + 1) * 64)
        for i, part in enumerate(gradients):
            moved = product(order, part[:, block * 128 : (block + 1) * 128], LAST).astype(BF)
            keep_ref[rows, i * 256 : (i + 1) * 256] = moved[:64]
            send_ref[rows, i * 256 : (i + 1) * 256] = moved[64:]
        done(block)


def weight_copies(refs, w_ref, sems, kinds):
    core, across, high = (lax.axis_index(name) for name in ("c", "x", "yh"))
    right = pl.ds(768, 256)
    pairs, sides = [], ([], [])
    for step in range(4):
        for flip in range(2):
            shard = ((across + 4 - step) & 3) * 2 + (high ^ flip)
            for side in range(2):
                ref = refs[4 * side + step].at[flip]
                half = core ^ side
                if kinds == 2:
                    pairs.append((ref, w_ref.at[half, shard]))
                else:
                    pairs.append((ref.at[:, right], w_ref.at[half, shard, :, right]))
                    left = pl.ds(0, 768)
                    sides[side].append((ref.at[:, left], w_ref.at[half, shard, :, left]))
    return pairs, sides


def kind_copies(kind, refs, w_ref, sems, first):
    pairs, sides = weight_copies(refs, w_ref, sems, 1)
    core = lax.axis_index("c")
    for side in range(2):

        @pl.when((core ^ side) == kind)
        def _(side=side):
            start_copies(sides[side], sems, first)

    waits = [
        pltpu.make_async_copy(source, target, sems.at[first + i])
        for i, (source, target) in enumerate(sides[0])
    ]
    return waits + start_copies(pairs, sems, first + 8)


def row_kernel(x_ref, ct_ref, bias_ref, *refs):
    weights, (parts_ref, keep_ref, send_ref, x_here, ct_here, bias, w_ref, sems) = refs[:8], refs[8:]
    copies = start_copies(((x_ref, x_here), (ct_ref, ct_here), (bias_ref, bias)), sems)
    more = kind_copies(0, weights, w_ref, sems, 3)
    wait_for(copies[:1])
    out, dq, dk, dv = attention(x_here, ct_here, w_ref, more + copies[1:], 0, bias)
    for i, part in enumerate((out, dq, dk, dv)):
        parts_ref[:, i * 256 : (i + 1) * 256] = part.T
    store_gradients(lax.axis_index("c"), x_here[...], ct_here[...], out, dv, keep_ref, send_ref)


def column_kernel(both_ref, bias_ref, *refs):
    weights, refs = refs[:8], refs[8:]
    parts_ref, keep_ref, send_ref, parts, keep, send, both, x, ct, bias, w_ref, sems = refs
    first = start_copies(((both_ref, both),), sems, 25)
    copies = kind_copies(1, weights, w_ref, sems, 1) + start_copies(((bias_ref, bias),), sems)
    wait_for(first)
    x[...], ct[...] = separate(both[...])
    out, dq, dk, dv = attention(x, ct, w_ref, copies, 1, bias)
    parts[:, 0:256] = interleave(out, dk, LAST)
    parts[:, 256:512] = interleave(dq, dv, LAST)
    stores = start_copies(((parts, parts_ref),), sems)


    def store(block):
        if block in (3, 7):
            rows = pl.ds((block - 3) * 64, 256)
            pairs = [(keep.at[rows], keep_ref.at[rows]), (send.at[rows], send_ref.at[rows])]
            stores.extend(start_copies(pairs, sems, block - 2))

    store_gradients(lax.axis_index("c"), x[...], ct[...], out, dv, keep, send, store)
    wait_for(stores)


def pick_kernel(row_keep, row_got, col_keep, col_got, *terms):
    across = lax.axis_index("x")
    for step, term in enumerate(terms):
        rows = pl.ds(pl.multiple_of(((across + step) & 3) * 128, 128), 128)
        for i, (keep, got) in enumerate(((row_keep, row_got), (col_keep, col_got))):
            total = keep[rows, :].astype(F32) + got[rows, :].astype(F32)
            term[:, i * 512 : (i + 1) * 512] = total.astype(BF)


def spread_kernel(*refs):
    given, keep_ref, send_ref, total = refs[:4], refs[4], refs[5], refs[6]
    total[...] = sum(ref[...].astype(F32) for ref in given).astype(BF)
    high = lax.axis_index("yh")
    keep_ref[...] = total[pl.ds(pl.multiple_of(high * 64, 64), 64), :]
    send_ref[...] = total[pl.ds(pl.multiple_of((high ^ 1) * 64, 64), 64), :]


def line_kernel(keep_ref, got_ref, out_ref):
    total = (keep_ref[...].astype(F32) + got_ref[...].astype(F32)).astype(BF)
    row = lax.broadcasted_iota(jnp.int32, (256, 64), 0)
    col = lax.broadcasted_iota(jnp.int32, (256, 64), 1)
    out = jnp.zeros((256, 256), F32)
    for b in range(4):
        here = (col == member(row >> 3, 2, BEGIN_LAST) * 2 + (row & 1)) & ((row & 6) == 2 * b)
        out += product(here.astype(F32).astype(BF), total[:, b * 256 : (b + 1) * 256])
    out_ref[...] = out.astype(BF)


def last_kernel(line_ref, value_ref, out_ref):
    total = jnp.sum(line_ref[...].astype(F32).reshape(32, 8, 256), axis=0)
    for kind in range(2):
        value_ref[:, kind * 256 : (kind + 1) * 256] = total[kind * 4 : kind * 4 + 2]
        out_ref[:, kind * 256 : (kind + 1) * 256] = total[kind * 4 + 2 : kind * 4 + 4]


def final_kernel(row_ref, col_ref, *refs):
    weights, (mixed_ref, gt_ref, row, w_ref, sems) = refs[:8], refs[8:]
    copies = start_copies(weight_copies(weights, w_ref, sems, 2)[0] + [(row_ref, row)], sems)
    first, second = separate(col_ref[...])
    wait_for(copies)
    sides = (
        (row[:, 0:256], row[:, 256:1024]),
        (first[:, 0:256], jnp.concatenate([first[:, 256:512], second], axis=1)),
    )
    for half in range(2):
        for b in range(2):
            total = jnp.zeros((256, 256), F32)
            for kind in range(2):
                block = w_ref[half, kind * 4 : kind * 4 + 4, b * 64 : (b + 1) * 64, 768:1024]
                total += product(sides[kind][0], block.reshape(256, 256))
            start = half * 512 + b * 256
            mixed_ref[:, start : start + 256] = total.astype(BF)
    total = jnp.zeros(gt_ref.shape, F32)
    for kind in range(2):
        total += product(sides[kind][1], w_ref[kind, :, :, 0:768].reshape(1024, 768), LAST)
    gt_ref[...] = total.astype(BF)


def shape(*dims):
    return jax.ShapeDtypeStruct(dims, BF)


def buffer(*dims):
    return pltpu.VMEM(dims, BF)


def cost(flops, moved):
    return pl.CostEstimate(flops=flops, bytes_accessed=moved, transcendentals=0)


def one_hot(index, size):
    return (index[:, None] == jnp.arange(size)[None, :]).astype(BF)


def biases(row_mask, column_mask):
    position = jnp.arange(256)
    seen = position[:, None] >= position[None, :]
    row_in = one_hot(position // ROWBLK, 2)
    row_blocks = jnp.einsum(
        "ia,hab,jb->hij", row_in, row_mask[:, 0].astype(BF), row_in, preferred_element_type=BF
    )
    same = (position[:, None] % 4) == (position[None, :] % 4)
    col_left = one_hot((position % 4) * 8 + position // (4 * COLBLK), 32)
    col_right = one_hot(position // (4 * COLBLK), 8)
    col_blocks = jnp.einsum(
        "ia,hab,jb->hij",
        col_left,
        column_mask.reshape(4, 32, 8).astype(BF),
        col_right,
        preferred_element_type=BF,
    )
    row_bias = jnp.where((row_blocks > 0.5) & seen, 0.0, MASKED).astype(BF)
    col_bias = jnp.where((col_blocks > 0.5) & seen & same, 0.0, MASKED).astype(BF)
    return row_bias, col_bias


def body(tokens, cotangent, row_mask, column_mask, w_query, w_key, w_value, w_out):
    flat = tokens.reshape(256, 1024)
    cot_flat = cotangent.reshape(256, 1024)
    seq = ("z", "yl", "c")

    sent = pl.pallas_call(
        interleave_kernel,
        out_shape=shape(512, 1024),
        in_specs=[VMEM] * 2,
        out_specs=HBM,
        scratch_shapes=[buffer(512, 1024), pltpu.SemaphoreType.DMA((4,))],
        compiler_params=room(16),
        cost_estimate=cost(540000000, 2000000),
        name="interleave",
    )(flat, cot_flat)
    packed = pl.pallas_call(
        pack_kernel,
        out_shape=shape(128, 1024),
        in_specs=[HBM] * 4,
        out_specs=VMEM,
        scratch_shapes=[pltpu.SemaphoreType.DMA((5,))],
        compiler_params=room(60),
        cost_estimate=cost(1000000000, 2000000),
        name="pack",
    )(w_query, w_key, w_value, w_out)
    with jax.named_scope("to_columns"):
        both = lax.all_to_all(
            sent.reshape(64, 8, 1024), seq, split_axis=0, concat_axis=0, tiled=True, axis_index_groups=groups(4, BEGIN)
        ).reshape(512, 1024)
    with jax.named_scope("masks"):
        row_bias, col_bias = biases(row_mask, column_mask)
    with jax.named_scope("weights"):
        flipped = lax.ppermute(packed, ("yh", "yl"), [(y, 3 - y) for y in range(4)])
        pair = pl.pallas_call(
            pair_kernel,
            out_shape=shape(2, 128, 1024),
            in_specs=[VMEM] * 2,
            out_specs=VMEM,
            compiler_params=room(16),
            cost_estimate=cost(PAIR, 1000000),
            name="pair",
        )(packed, flipped)
        weights = [pair] + [
            lax.ppermute(pair, "x", [(x, (x + step) % 4) for x in range(4)]) for step in (1, 2, 3)
        ]
        weights[3], row_bias, col_bias = lax.optimization_barrier((weights[3], row_bias, col_bias))
        weights += [lax.ppermute(part, "c", SWAP) for part in weights]
    row_parts, row_keep, row_send = pl.pallas_call(
        row_kernel,
        out_shape=(shape(256, 1024), shape(512, 512), shape(512, 512)),
        in_specs=[HBM] * 11,
        out_specs=(VMEM,) * 3,
        scratch_shapes=[
            buffer(256, 1024),
            buffer(256, 1024),
            buffer(4, 256, 256),
            buffer(2, 8, 128, 1024),
            pltpu.SemaphoreType.DMA((27,)),
        ],
        compiler_params=room(58),
        cost_estimate=cost(1400000000, 12000000),
        name="row_heads",
    )(flat, cot_flat, row_bias, *weights)
    row_got = lax.ppermute(row_send, "c", SWAP)
    both, row_keep = lax.optimization_barrier((both, row_keep))
    col_parts, col_keep, col_send = pl.pallas_call(
        column_kernel,
        out_shape=(shape(512, 512),) * 3,
        in_specs=[HBM] * 10,
        out_specs=(HBM,) * 3,
        scratch_shapes=[
            buffer(512, 512),
            buffer(512, 512),
            buffer(512, 512),
            buffer(512, 1024),
            buffer(256, 1024),
            buffer(256, 1024),
            buffer(4, 256, 256),
            buffer(2, 8, 128, 1024),
            pltpu.SemaphoreType.DMA((26,)),
        ],
        compiler_params=room(58),
        cost_estimate=cost(1900000000, 8000000),
        name="column_heads",
    )(both, col_bias, *weights)
    col_got = lax.ppermute(col_send, "c", SWAP)
    with jax.named_scope("from_columns"):
        returned = lax.all_to_all(
            col_parts.reshape(64, 8, 512), seq, split_axis=0, concat_axis=0, tiled=True, axis_index_groups=groups(4, BEGIN)
        ).reshape(512, 512)

    with jax.named_scope("gradient_sums"):
        terms = pl.pallas_call(
            pick_kernel,
            out_shape=(shape(128, 1024),) * 4,
            in_specs=[VMEM] * 4,
            out_specs=(VMEM,) * 4,
            compiler_params=room(16),
            cost_estimate=cost(PICK, 3000000),
            name="pick",
        )(row_keep, row_got, col_keep, col_got)
        moved = [
            lax.ppermute(terms[step], "x", [(x, (x + step) % 4) for x in range(4)])
            for step in (2, 1, 3)
        ]
        line_keep, line_send = pl.pallas_call(
            spread_kernel,
            out_shape=(shape(64, 1024),) * 2,
            in_specs=[VMEM] * 4,
            out_specs=(VMEM,) * 2,
            scratch_shapes=[buffer(128, 1024)],
            compiler_params=room(16),
            cost_estimate=cost(10000000, 1000000),
            name="spread",
        )(terms[0], *moved)
        line_got = lax.ppermute(line_send, ("yh", "yl"), [(y, 3 - y) for y in range(4)])
        line = pl.pallas_call(
            line_kernel,
            out_shape=shape(256, 256),
            in_specs=[VMEM] * 2,
            out_specs=VMEM,
            compiler_params=room(16),
            cost_estimate=cost(10000000, 300000),
            name="line",
        )(line_keep, line_got)
        line, returned = lax.optimization_barrier((line, returned))
        line = lax.all_to_all(
            line.reshape(32, 8, 256), ("z", "yl"), split_axis=0, concat_axis=0, tiled=True, axis_index_groups=groups(2, BEGIN_LAST)
        )
        grad_value, grad_output = pl.pallas_call(
            last_kernel,
            out_shape=(jax.ShapeDtypeStruct((2, 512), F32),) * 2,
            in_specs=[VMEM],
            out_specs=(VMEM,) * 2,
            compiler_params=room(16),
            cost_estimate=cost(100000, 100000),
            name="last",
        )(line.reshape(256, 256))
        grad_output = jnp.transpose(grad_output)
    mixed, grad_tokens = pl.pallas_call(
        final_kernel,
        out_shape=(shape(256, 1024), shape(256, 1024)),
        in_specs=[HBM, VMEM] + [HBM] * 8,
        out_specs=(VMEM, VMEM),
        scratch_shapes=[
            buffer(256, 1024),
            buffer(2, 8, 128, 1024),
            pltpu.SemaphoreType.DMA((17,)),
        ],
        compiler_params=room(58),
        cost_estimate=cost(1200000000, 8000000),
        name="output_products",
    )(row_parts, returned, *weights)
    return (
        mixed.reshape(tokens.shape),
        grad_tokens.reshape(tokens.shape),
        grad_value,
        grad_output,
    )


def solution(mesh):
    fine = Mesh(mesh.devices.reshape(4, 2, 16, 2, 2), ("x", "yh", "z", "yl", "c"))
    dp, seq = ("x", "yh"), ("z", "yl", "c")
    return jax.shard_map(
        body,
        mesh=fine,
        in_specs=(
            P(dp, seq, None, None),
            P(dp, seq, None, None),
            P(None, seq, None, None),
            P(None, seq, None, None),
            P(dp, None),
            P(dp, None),
            P(dp, None),
            P(dp, None),
        ),
        out_specs=(
            P(dp, seq, None, None),
            P(dp, seq, None, None),
            P(dp + seq, None),
            P(None, dp + seq),
        ),
        check_vma=False,
    )
```

```python
import functools

import jax
import jax.numpy as jnp
from jax import lax
from jax.experimental import pallas as pl
from jax.experimental.pallas import tpu as pltpu
from jax.sharding import Mesh, PartitionSpec as P

HEAD_DIM = 64
ROWBLK = 128
COLBLK = 8
BF = jnp.bfloat16
F32 = jnp.float32
LAST = (((1,), (1,)), ((), ()))
FIRST = (((0,), (0,)), ((), ()))
MASKED = -1e30
VMEM = pl.BlockSpec(memory_space=pltpu.VMEM)
HBM = pl.BlockSpec(memory_space=pltpu.HBM)


def room(mebibytes):
    return pltpu.CompilerParams(vmem_limit_bytes=mebibytes * 1024 * 1024)


SWAP = [(0, 1), (1, 0)]
BEGIN, BEGIN_LAST = 10, 8
PAIR, PICK = 30000000000, 14000000000


def product(a, b, dims=(((1,), (0,)), ((), ()))):
    return lax.dot_general(a, b, dims, preferred_element_type=F32)


def member(place, rest, begin):
    return (place + begin * rest) & (16 * rest - 1)


def groups(rest, begin):
    return [[member(place, rest, begin) for place in range(16 * rest)]]


def eights(first, start=0, rows=512):
    row = lax.broadcasted_iota(jnp.int32, (rows, 256), 0) + start
    col = lax.broadcasted_iota(jnp.int32, (rows, 256), 1)
    inside = (row & 4) == (0 if first else 4)
    return ((col == member(row >> 3, 4, BEGIN) * 4 + (row & 3)) & inside).astype(F32).astype(BF)


def interleave(first, second, dims=(((1,), (0,)), ((), ())), start=0, rows=512):
    return (
        product(eights(True, start, rows), first, dims)
        + product(eights(False, start, rows), second, dims)
    ).astype(BF)


def separate(both):
    return tuple(product(eights(t), both, FIRST).astype(BF) for t in (True, False))


def start_copies(pairs, sems, first=0):
    copies = [
        pltpu.make_async_copy(source, target, sems.at[first + i])
        for i, (source, target) in enumerate(pairs)
    ]
    for copy in copies:
        copy.start()
    return copies


def wait_for(copies):
    for copy in copies:
        copy.wait()


def interleave_kernel(x_ref, ct_ref, sent_ref, sent, sems):
    stores = []
    for i in range(4):
        out = pl.ds(i * 128, 128)
        sent[out] = interleave(x_ref[...], ct_ref[...], start=i * 128, rows=128)
        stores += start_copies([(sent.at[out], sent_ref.at[out])], sems, i)
    wait_for(stores)


def pack_kernel(wq_ref, wk_ref, wv_ref, wo_ref, packed_ref, sems):
    core = lax.axis_index("c")
    here = pl.ds(pl.multiple_of(core * 256, 256), 256)
    pairs = []
    for i, ref in enumerate((wq_ref, wk_ref, wv_ref)):
        pairs.append((ref.at[:, here], packed_ref.at[:, pl.ds(i * 256, 256)]))
    for b in range(2):
        there = pl.ds(pl.multiple_of(core * 512 + b * 256, 256), 256)
        pairs.append((wo_ref.at[:, there], packed_ref.at[pl.ds(b * 64, 64), pl.ds(768, 256)]))
    wait_for(start_copies(pairs, sems))


def pair_kernel(packed_ref, flipped_ref, pair_ref):
    pair_ref[0] = packed_ref[...]
    pair_ref[1] = flipped_ref[...]


def attention(x_ref, ct_ref, weights, copies, kind, bias_ref):
    across = lax.axis_index("x")
    qkv = jnp.zeros((256, 768), F32)
    for step in range(4):
        wait_for(copies[2 * step : 2 * step + 2])
        source = (across + 4 - step) & 3
        left = x_ref[:, pl.ds(pl.multiple_of(source * 256, 256), 256)]
        qkv += product(left, weights[kind, pl.ds(source * 2, 2), :, 0:768].reshape(256, 768))
    qkv = qkv.astype(BF)
    q, k, v = qkv[:, :256], qkv[:, 256:512], qkv[:, 512:]
    wait_for(copies[8:])
    ct = ct_ref[...]
    do = jnp.zeros((256, 256), F32)
    for half in range(2):
        for b in range(2):
            block = weights[half, kind * 4 : kind * 4 + 4, b * 64 : (b + 1) * 64, 768:1024]
            start = half * 512 + b * 256
            do += product(ct[:, start : start + 256], block.reshape(256, 256), LAST)
    do = do.astype(BF)
    q = q * jnp.asarray(0.125, BF)
    qt, kt, vt, ot = q.T, (k * jnp.asarray(0.125, BF)).T, v.T, do.T
    lane = lax.broadcasted_iota(jnp.int32, (256, 256), 1) // HEAD_DIM
    zero = jnp.zeros_like(q)
    heads = range(4)
    s = [product(jnp.where(lane == h, q, zero), k, LAST) + bias_ref[h].astype(F32) for h in heads]
    e = [jnp.exp(a - jnp.max(a, axis=-1, keepdims=True)) for a in s]
    w = [a * (1.0 / jnp.sum(a, axis=-1, keepdims=True)) for a in e]
    p = [a.astype(BF) for a in w]
    dp = [product(jnp.where(lane == h, do, zero), v, LAST) for h in heads]
    ds = [(a * (b - jnp.sum(b * a, axis=-1, keepdims=True))).astype(BF) for a, b in zip(w, dp)]
    rows = [slice(h * HEAD_DIM, (h + 1) * HEAD_DIM) for h in heads]
    results = (
        [product(vt[rows[h]], p[h], LAST) for h in heads],
        [product(kt[rows[h]], ds[h], LAST) for h in heads],
        [product(qt[rows[h]], ds[h]) for h in heads],
        [product(ot[rows[h]], p[h]) for h in heads],
    )
    return tuple(jnp.concatenate(a, axis=0).astype(BF) for a in results)


def store_gradients(core, x, ct, outt, dvt, keep_ref, send_ref, done=lambda block: None):
    gradients = (product(dvt, x).astype(BF), product(outt, ct).astype(BF))
    new = lax.broadcasted_iota(jnp.int32, (128, 128), 0)
    old = lax.broadcasted_iota(jnp.int32, (128, 128), 1)
    source = ((new >> 1) & 31) * 4 + ((new >> 6) ^ core) * 2 + (new & 1)
    order = (old == source).astype(F32).astype(BF)
    for block in range(8):
        rows = slice(block * 64, (block + 1) * 64)
        for i, part in enumerate(gradients):
            moved = product(order, part[:, block * 128 : (block + 1) * 128], LAST).astype(BF)
            keep_ref[rows, i * 256 : (i + 1) * 256] = moved[:64]
            send_ref[rows, i * 256 : (i + 1) * 256] = moved[64:]
        done(block)


def weight_copies(refs, w_ref, sems, kinds):
    core, across, high = (lax.axis_index(name) for name in ("c", "x", "yh"))
    right = pl.ds(768, 256)
    pairs, sides = [], ([], [])
    for step in range(4):
        for flip in range(2):
            shard = ((across + 4 - step) & 3) * 2 + (high ^ flip)
            for side in range(2):
                ref = refs[4 * side + step].at[flip]
                half = core ^ side
                if kinds == 2:
                    pairs.append((ref, w_ref.at[half, shard]))
                else:
                    pairs.append((ref.at[:, right], w_ref.at[half, shard, :, right]))
                    left = pl.ds(0, 768)
                    sides[side].append((ref.at[:, left], w_ref.at[half, shard, :, left]))
    return pairs, sides


def kind_copies(kind, refs, w_ref, sems, first):
    pairs, sides = weight_copies(refs, w_ref, sems, 1)
    core = lax.axis_index("c")
    for side in range(2):

        @pl.when((core ^ side) == kind)
        def _(side=side):
            start_copies(sides[side], sems, first)

    waits = [
        pltpu.make_async_copy(source, target, sems.at[first + i])
        for i, (source, target) in enumerate(sides[0])
    ]
    return waits + start_copies(pairs, sems, first + 8)


def row_kernel(x_ref, ct_ref, bias_ref, *refs):
    weights, (parts_ref, keep_ref, send_ref, x_here, ct_here, bias, w_ref, sems) = refs[:8], refs[8:]
    copies = start_copies(((x_ref, x_here), (ct_ref, ct_here), (bias_ref, bias)), sems)
    more = kind_copies(0, weights, w_ref, sems, 3)
    wait_for(copies[:1])
    out, dq, dk, dv = attention(x_here, ct_here, w_ref, more + copies[1:], 0, bias)
    for i, part in enumerate((out, dq, dk, dv)):
        parts_ref[:, i * 256 : (i + 1) * 256] = part.T
    store_gradients(lax.axis_index("c"), x_here[...], ct_here[...], out, dv, keep_ref, send_ref)


def column_kernel(both_ref, bias_ref, *refs):
    weights, refs = refs[:8], refs[8:]
    parts_ref, keep_ref, send_ref, parts, keep, send, both, x, ct, bias, w_ref, sems = refs
    first = start_copies(((both_ref, both),), sems, 25)
    copies = kind_copies(1, weights, w_ref, sems, 1) + start_copies(((bias_ref, bias),), sems)
    wait_for(first)
    x[...], ct[...] = separate(both[...])
    out, dq, dk, dv = attention(x, ct, w_ref, copies, 1, bias)
    parts[:, 0:256] = interleave(out, dk, LAST)
    parts[:, 256:512] = interleave(dq, dv, LAST)
    stores = start_copies(((parts, parts_ref),), sems)


    def store(block):
        if block in (3, 7):
            rows = pl.ds((block - 3) * 64, 256)
            pairs = [(keep.at[rows], keep_ref.at[rows]), (send.at[rows], send_ref.at[rows])]
            stores.extend(start_copies(pairs, sems, block - 2))

    store_gradients(lax.axis_index("c"), x[...], ct[...], out, dv, keep, send, store)
    wait_for(stores)


def pick_kernel(row_keep, row_got, col_keep, col_got, *terms):
    across = lax.axis_index("x")
    for step, term in enumerate(terms):
        rows = pl.ds(pl.multiple_of(((across + step) & 3) * 128, 128), 128)
        for i, (keep, got) in enumerate(((row_keep, row_got), (col_keep, col_got))):
            total = keep[rows, :].astype(F32) + got[rows, :].astype(F32)
            term[:, i * 512 : (i + 1) * 512] = total.astype(BF)


def spread_kernel(*refs):
    given, keep_ref, send_ref, total = refs[:4], refs[4], refs[5], refs[6]
    total[...] = sum(ref[...].astype(F32) for ref in given).astype(BF)
    high = lax.axis_index("yh")
    keep_ref[...] = total[pl.ds(pl.multiple_of(high * 64, 64), 64), :]
    send_ref[...] = total[pl.ds(pl.multiple_of((high ^ 1) * 64, 64), 64), :]


def line_kernel(keep_ref, got_ref, out_ref):
    total = (keep_ref[...].astype(F32) + got_ref[...].astype(F32)).astype(BF)
    row = lax.broadcasted_iota(jnp.int32, (256, 64), 0)
    col = lax.broadcasted_iota(jnp.int32, (256, 64), 1)
    out = jnp.zeros((256, 256), F32)
    for b in range(4):
        here = (col == member(row >> 3, 2, BEGIN_LAST) * 2 + (row & 1)) & ((row & 6) == 2 * b)
        out += product(here.astype(F32).astype(BF), total[:, b * 256 : (b + 1) * 256])
    out_ref[...] = out.astype(BF)


def last_kernel(line_ref, value_ref, out_ref):
    total = jnp.sum(line_ref[...].astype(F32).reshape(32, 8, 256), axis=0)
    for kind in range(2):
        value_ref[:, kind * 256 : (kind + 1) * 256] = total[kind * 4 : kind * 4 + 2]
        out_ref[:, kind * 256 : (kind + 1) * 256] = total[kind * 4 + 2 : kind * 4 + 4]


def final_kernel(row_ref, col_ref, *refs):
    weights, (mixed_ref, gt_ref, row, w_ref, sems) = refs[:8], refs[8:]
    copies = start_copies(weight_copies(weights, w_ref, sems, 2)[0] + [(row_ref, row)], sems)
    first, second = separate(col_ref[...])
    wait_for(copies)
    sides = (
        (row[:, 0:256], row[:, 256:1024]),
        (first[:, 0:256], jnp.concatenate([first[:, 256:512], second], axis=1)),
    )
    for half in range(2):
        for b in range(2):
            total = jnp.zeros((256, 256), F32)
            for kind in range(2):
                block = w_ref[half, kind * 4 : kind * 4 + 4, b * 64 : (b + 1) * 64, 768:1024]
                total += product(sides[kind][0], block.reshape(256, 256))
            start = half * 512 + b * 256
            mixed_ref[:, start : start + 256] = total.astype(BF)
    total = jnp.zeros(gt_ref.shape, F32)
    for kind in range(2):
        total += product(sides[kind][1], w_ref[kind, :, :, 0:768].reshape(1024, 768), LAST)
    gt_ref[...] = total.astype(BF)


def shape(*dims):
    return jax.ShapeDtypeStruct(dims, BF)


def buffer(*dims):
    return pltpu.VMEM(dims, BF)


def cost(flops, moved):
    return pl.CostEstimate(flops=flops, bytes_accessed=moved, transcendentals=0)


def one_hot(index, size):
    return (index[:, None] == jnp.arange(size)[None, :]).astype(BF)


def biases(row_mask, column_mask):
    position = jnp.arange(256)
    seen = position[:, None] >= position[None, :]
    row_in = one_hot(position // ROWBLK, 2)
    row_blocks = jnp.einsum(
        "ia,hab,jb->hij", row_in, row_mask[:, 0].astype(BF), row_in, preferred_element_type=BF
    )
    same = (position[:, None] % 4) == (position[None, :] % 4)
    col_left = one_hot((position % 4) * 8 + position // (4 * COLBLK), 32)
    col_right = one_hot(position // (4 * COLBLK), 8)
    col_blocks = jnp.einsum(
        "ia,hab,jb->hij",
        col_left,
        column_mask.reshape(4, 32, 8).astype(BF),
        col_right,
        preferred_element_type=BF,
    )
    row_bias = jnp.where((row_blocks > 0.5) & seen, 0.0, MASKED).astype(BF)
    col_bias = jnp.where((col_blocks > 0.5) & seen & same, 0.0, MASKED).astype(BF)
    return row_bias, col_bias


def body(tokens, cotangent, row_mask, column_mask, w_query, w_key, w_value, w_out):
    flat = tokens.reshape(256, 1024)
    cot_flat = cotangent.reshape(256, 1024)
    seq = ("z", "yl", "c")

    sent = pl.pallas_call(
        interleave_kernel,
        out_shape=shape(512, 1024),
        in_specs=[VMEM] * 2,
        out_specs=HBM,
        scratch_shapes=[buffer(512, 1024), pltpu.SemaphoreType.DMA((4,))],
        compiler_params=room(16),
        cost_estimate=cost(540000000, 2000000),
        name="interleave",
    )(flat, cot_flat)
    packed = pl.pallas_call(
        pack_kernel,
        out_shape=shape(128, 1024),
        in_specs=[HBM] * 4,
        out_specs=VMEM,
        scratch_shapes=[pltpu.SemaphoreType.DMA((5,))],
        compiler_params=room(60),
        cost_estimate=cost(1000000000, 2000000),
        name="pack",
    )(w_query, w_key, w_value, w_out)
    with jax.named_scope("to_columns"):
        both = lax.all_to_all(
            sent.reshape(64, 8, 1024), seq, split_axis=0, concat_axis=0, tiled=True, axis_index_groups=groups(4, BEGIN)
        ).reshape(512, 1024)
    with jax.named_scope("masks"):
        row_bias, col_bias = biases(row_mask, column_mask)
    with jax.named_scope("weights"):
        flipped = lax.ppermute(packed, ("yh", "yl"), [(y, 3 - y) for y in range(4)])
        pair = pl.pallas_call(
            pair_kernel,
            out_shape=shape(2, 128, 1024),
            in_specs=[VMEM] * 2,
            out_specs=VMEM,
            compiler_params=room(16),
            cost_estimate=cost(PAIR, 1000000),
            name="pair",
        )(packed, flipped)
        weights = [pair] + [
            lax.ppermute(pair, "x", [(x, (x + step) % 4) for x in range(4)]) for step in (1, 2, 3)
        ]
        weights[3], row_bias, col_bias = lax.optimization_barrier((weights[3], row_bias, col_bias))
        weights += [lax.ppermute(part, "c", SWAP) for part in weights]
    row_parts, row_keep, row_send = pl.pallas_call(
        row_kernel,
        out_shape=(shape(256, 1024), shape(512, 512), shape(512, 512)),
        in_specs=[HBM] * 11,
        out_specs=(VMEM,) * 3,
        scratch_shapes=[
            buffer(256, 1024),
            buffer(256, 1024),
            buffer(4, 256, 256),
            buffer(2, 8, 128, 1024),
            pltpu.SemaphoreType.DMA((27,)),
        ],
        compiler_params=room(58),
        cost_estimate=cost(1400000000, 12000000),
        name="row_heads",
    )(flat, cot_flat, row_bias, *weights)
    row_got = lax.ppermute(row_send, "c", SWAP)
    both, row_keep = lax.optimization_barrier((both, row_keep))
    col_parts, col_keep, col_send = pl.pallas_call(
        column_kernel,
        out_shape=(shape(512, 512),) * 3,
        in_specs=[HBM] * 10,
        out_specs=(HBM,) * 3,
        scratch_shapes=[
            buffer(512, 512),
            buffer(512, 512),
            buffer(512, 512),
            buffer(512, 1024),
            buffer(256, 1024),
            buffer(256, 1024),
            buffer(4, 256, 256),
            buffer(2, 8, 128, 1024),
            pltpu.SemaphoreType.DMA((26,)),
        ],
        compiler_params=room(58),
        cost_estimate=cost(1900000000, 8000000),
        name="column_heads",
    )(both, col_bias, *weights)
    col_got = lax.ppermute(col_send, "c", SWAP)
    with jax.named_scope("from_columns"):
        returned = lax.all_to_all(
            col_parts.reshape(64, 8, 512), seq, split_axis=0, concat_axis=0, tiled=True, axis_index_groups=groups(4, BEGIN)
        ).reshape(512, 512)

    with jax.named_scope("gradient_sums"):
        terms = pl.pallas_call(
            pick_kernel,
            out_shape=(shape(128, 1024),) * 4,
            in_specs=[VMEM] * 4,
            out_specs=(VMEM,) * 4,
            compiler_params=room(16),
            cost_estimate=cost(PICK, 3000000),
            name="pick",
        )(row_keep, row_got, col_keep, col_got)
        moved = [
            lax.ppermute(terms[step], "x", [(x, (x + step) % 4) for x in range(4)])
            for step in (2, 1, 3)
        ]
        line_keep, line_send = pl.pallas_call(
            spread_kernel,
            out_shape=(shape(64, 1024),) * 2,
            in_specs=[VMEM] * 4,
            out_specs=(VMEM,) * 2,
            scratch_shapes=[buffer(128, 1024)],
            compiler_params=room(16),
            cost_estimate=cost(10000000, 1000000),
            name="spread",
        )(terms[0], *moved)
        line_got = lax.ppermute(line_send, ("yh", "yl"), [(y, 3 - y) for y in range(4)])
        line = pl.pallas_call(
            line_kernel,
            out_shape=shape(256, 256),
            in_specs=[VMEM] * 2,
            out_specs=VMEM,
            compiler_params=room(16),
            cost_estimate=cost(10000000, 300000),
            name="line",
        )(line_keep, line_got)
        line, returned = lax.optimization_barrier((line, returned))
        line = lax.all_to_all(
            line.reshape(32, 8, 256), ("z", "yl"), split_axis=0, concat_axis=0, tiled=True, axis_index_groups=groups(2, BEGIN_LAST)
        )
        grad_value, grad_output = pl.pallas_call(
            last_kernel,
            out_shape=(jax.ShapeDtypeStruct((2, 512), F32),) * 2,
            in_specs=[VMEM],
            out_specs=(VMEM,) * 2,
            compiler_params=room(16),
            cost_estimate=cost(100000, 100000),
            name="last",
        )(line.reshape(256, 256))
        grad_output = jnp.transpose(grad_output)
    mixed, grad_tokens = pl.pallas_call(
        final_kernel,
        out_shape=(shape(256, 1024), shape(256, 1024)),
        in_specs=[HBM, VMEM] + [HBM] * 8,
        out_specs=(VMEM, VMEM),
        scratch_shapes=[
            buffer(256, 1024),
            buffer(2, 8, 128, 1024),
            pltpu.SemaphoreType.DMA((17,)),
        ],
        compiler_params=room(58),
        cost_estimate=cost(1200000000, 8000000),
        name="output_products",
    )(row_parts, returned, *weights)
    return (
        mixed.reshape(tokens.shape),
        grad_tokens.reshape(tokens.shape),
        grad_value,
        grad_output,
    )


def solution(mesh):
    fine = Mesh(mesh.devices.reshape(4, 2, 16, 2, 2), ("x", "yh", "z", "yl", "c"))
    dp, seq = ("x", "yh"), ("z", "yl", "c")
    return jax.shard_map(
        body,
        mesh=fine,
        in_specs=(
            P(dp, seq, None, None),
            P(dp, seq, None, None),
            P(None, seq, None, None),
            P(None, seq, None, None),
            P(dp, None),
            P(dp, None),
            P(dp, None),
            P(dp, None),
        ),
        out_specs=(
            P(dp, seq, None, None),
            P(dp, seq, None, None),
            P(dp + seq, None),
            P(None, dp + seq),
        ),
        check_vma=False,
    )
```

```python
import functools

import jax
import jax.numpy as jnp
from jax import lax
from jax.experimental import pallas as pl
from jax.experimental.pallas import tpu as pltpu
from jax.sharding import Mesh, PartitionSpec as P

HEAD_DIM = 64
ROWBLK = 128
COLBLK = 8
BF = jnp.bfloat16
F32 = jnp.float32
LAST = (((1,), (1,)), ((), ()))
FIRST = (((0,), (0,)), ((), ()))
MASKED = -1e30
VMEM = pl.BlockSpec(memory_space=pltpu.VMEM)
HBM = pl.BlockSpec(memory_space=pltpu.HBM)


def room(mebibytes):
    return pltpu.CompilerParams(vmem_limit_bytes=mebibytes * 1024 * 1024)


SWAP = [(0, 1), (1, 0)]
BEGIN, BEGIN_LAST = 10, 8
PAIR, PICK = 30000000000, 14000000000


def product(a, b, dims=(((1,), (0,)), ((), ()))):
    return lax.dot_general(a, b, dims, preferred_element_type=F32)


def member(place, rest, begin):
    return (place + begin * rest) & (16 * rest - 1)


def groups(rest, begin):
    return [[member(place, rest, begin) for place in range(16 * rest)]]


def eights(first, start=0, rows=512):
    row = lax.broadcasted_iota(jnp.int32, (rows, 256), 0) + start
    col = lax.broadcasted_iota(jnp.int32, (rows, 256), 1)
    inside = (row & 4) == (0 if first else 4)
    return ((col == member(row >> 3, 4, BEGIN) * 4 + (row & 3)) & inside).astype(F32).astype(BF)


def interleave(first, second, dims=(((1,), (0,)), ((), ())), start=0, rows=512):
    return (
        product(eights(True, start, rows), first, dims)
        + product(eights(False, start, rows), second, dims)
    ).astype(BF)


def separate(both):
    return tuple(product(eights(t), both, FIRST).astype(BF) for t in (True, False))


def start_copies(pairs, sems, first=0):
    copies = [
        pltpu.make_async_copy(source, target, sems.at[first + i])
        for i, (source, target) in enumerate(pairs)
    ]
    for copy in copies:
        copy.start()
    return copies


def wait_for(copies):
    for copy in copies:
        copy.wait()


def interleave_kernel(x_ref, ct_ref, sent_ref, sent, sems):
    stores = []
    for i in range(4):
        out = pl.ds(i * 128, 128)
        sent[out] = interleave(x_ref[...], ct_ref[...], start=i * 128, rows=128)
        stores += start_copies([(sent.at[out], sent_ref.at[out])], sems, i)
    wait_for(stores)


def pack_kernel(wq_ref, wk_ref, wv_ref, wo_ref, packed_ref, sems):
    core = lax.axis_index("c")
    here = pl.ds(pl.multiple_of(core * 256, 256), 256)
    pairs = []
    for i, ref in enumerate((wq_ref, wk_ref, wv_ref)):
        pairs.append((ref.at[:, here], packed_ref.at[:, pl.ds(i * 256, 256)]))
    for b in range(2):
        there = pl.ds(pl.multiple_of(core * 512 + b * 256, 256), 256)
        pairs.append((wo_ref.at[:, there], packed_ref.at[pl.ds(b * 64, 64), pl.ds(768, 256)]))
    wait_for(start_copies(pairs, sems))


def pair_kernel(packed_ref, flipped_ref, pair_ref):
    pair_ref[0] = packed_ref[...]
    pair_ref[1] = flipped_ref[...]


def attention(x_ref, ct_ref, weights, copies, kind, bias_ref):
    across = lax.axis_index("x")
    qkv = jnp.zeros((256, 768), F32)
    for step in range(4):
        wait_for(copies[2 * step : 2 * step + 2])
        source = (across + 4 - step) & 3
        left = x_ref[:, pl.ds(pl.multiple_of(source * 256, 256), 256)]
        qkv += product(left, weights[kind, pl.ds(source * 2, 2), :, 0:768].reshape(256, 768))
    qkv = qkv.astype(BF)
    q, k, v = qkv[:, :256], qkv[:, 256:512], qkv[:, 512:]
    wait_for(copies[8:])
    ct = ct_ref[...]
    do = jnp.zeros((256, 256), F32)
    for half in range(2):
        for b in range(2):
            block = weights[half, kind * 4 : kind * 4 + 4, b * 64 : (b + 1) * 64, 768:1024]
            start = half * 512 + b * 256
            do += product(ct[:, start : start + 256], block.reshape(256, 256), LAST)
    do = do.astype(BF)
    q = q * jnp.asarray(0.125, BF)
    qt, kt, vt, ot = q.T, (k * jnp.asarray(0.125, BF)).T, v.T, do.T
    lane = lax.broadcasted_iota(jnp.int32, (256, 256), 1) // HEAD_DIM
    zero = jnp.zeros_like(q)
    heads = range(4)
    s = [product(jnp.where(lane == h, q, zero), k, LAST) + bias_ref[h].astype(F32) for h in heads]
    e = [jnp.exp(a - jnp.max(a, axis=-1, keepdims=True)) for a in s]
    w = [a * (1.0 / jnp.sum(a, axis=-1, keepdims=True)) for a in e]
    p = [a.astype(BF) for a in w]
    dp = [product(jnp.where(lane == h, do, zero), v, LAST) for h in heads]
    ds = [(a * (b - jnp.sum(b * a, axis=-1, keepdims=True))).astype(BF) for a, b in zip(w, dp)]
    rows = [slice(h * HEAD_DIM, (h + 1) * HEAD_DIM) for h in heads]
    results = (
        [product(vt[rows[h]], p[h], LAST) for h in heads],
        [product(kt[rows[h]], ds[h], LAST) for h in heads],
        [product(qt[rows[h]], ds[h]) for h in heads],
        [product(ot[rows[h]], p[h]) for h in heads],
    )
    return tuple(jnp.concatenate(a, axis=0).astype(BF) for a in results)


def store_gradients(core, x, ct, outt, dvt, keep_ref, send_ref, done=lambda block: None):
    gradients = (product(dvt, x).astype(BF), product(outt, ct).astype(BF))
    new = lax.broadcasted_iota(jnp.int32, (128, 128), 0)
    old = lax.broadcasted_iota(jnp.int32, (128, 128), 1)
    source = ((new >> 1) & 31) * 4 + ((new >> 6) ^ core) * 2 + (new & 1)
    order = (old == source).astype(F32).astype(BF)
    for block in range(8):
        rows = slice(block * 64, (block + 1) * 64)
        for i, part in enumerate(gradients):
            moved = product(order, part[:, block * 128 : (block + 1) * 128], LAST).astype(BF)
            keep_ref[rows, i * 256 : (i + 1) * 256] = moved[:64]
            send_ref[rows, i * 256 : (i + 1) * 256] = moved[64:]
        done(block)


def weight_copies(refs, w_ref, sems, kinds):
    core, across, high = (lax.axis_index(name) for name in ("c", "x", "yh"))
    right = pl.ds(768, 256)
    pairs, sides = [], ([], [])
    for step in range(4):
        for flip in range(2):
            shard = ((across + 4 - step) & 3) * 2 + (high ^ flip)
            for side in range(2):
                ref = refs[4 * side + step].at[flip]
                half = core ^ side
                if kinds == 2:
                    pairs.append((ref, w_ref.at[half, shard]))
                else:
                    pairs.append((ref.at[:, right], w_ref.at[half, shard, :, right]))
                    left = pl.ds(0, 768)
                    sides[side].append((ref.at[:, left], w_ref.at[half, shard, :, left]))
    return pairs, sides


def kind_copies(kind, refs, w_ref, sems, first):
    pairs, sides = weight_copies(refs, w_ref, sems, 1)
    core = lax.axis_index("c")
    for side in range(2):

        @pl.when((core ^ side) == kind)
        def _(side=side):
            start_copies(sides[side], sems, first)

    waits = [
        pltpu.make_async_copy(source, target, sems.at[first + i])
        for i, (source, target) in enumerate(sides[0])
    ]
    return waits + start_copies(pairs, sems, first + 8)


def row_kernel(x_ref, ct_ref, bias_ref, *refs):
    weights, (parts_ref, keep_ref, send_ref, x_here, ct_here, bias, w_ref, sems) = refs[:8], refs[8:]
    copies = start_copies(((x_ref, x_here), (ct_ref, ct_here), (bias_ref, bias)), sems)
    more = kind_copies(0, weights, w_ref, sems, 3)
    wait_for(copies[:1])
    out, dq, dk, dv = attention(x_here, ct_here, w_ref, more + copies[1:], 0, bias)
    for i, part in enumerate((out, dq, dk, dv)):
        parts_ref[:, i * 256 : (i + 1) * 256] = part.T
    store_gradients(lax.axis_index("c"), x_here[...], ct_here[...], out, dv, keep_ref, send_ref)


def column_kernel(both_ref, bias_ref, *refs):
    weights, refs = refs[:8], refs[8:]
    parts_ref, keep_ref, send_ref, parts, keep, send, both, x, ct, bias, w_ref, sems = refs
    first = start_copies(((both_ref, both),), sems, 25)
    copies = kind_copies(1, weights, w_ref, sems, 1) + start_copies(((bias_ref, bias),), sems)
    wait_for(first)
    x[...], ct[...] = separate(both[...])
    out, dq, dk, dv = attention(x, ct, w_ref, copies, 1, bias)
    parts[:, 0:256] = interleave(out, dk, LAST)
    parts[:, 256:512] = interleave(dq, dv, LAST)
    stores = start_copies(((parts, parts_ref),), sems)


    def store(block):
        if block in (3, 5, 7):
            first = {3: 0, 5: 256, 7: 384}[block]
            rows = pl.ds(first, (block + 1) * 64 - first)
            pairs = [(send.at[rows], send_ref.at[rows]), (keep.at[rows], keep_ref.at[rows])]
            stores.extend(start_copies(pairs, sems, block - 2))

    store_gradients(lax.axis_index("c"), x[...], ct[...], out, dv, keep, send, store)
    wait_for(stores)


def pick_kernel(row_keep, row_got, col_keep, col_got, *terms):
    across = lax.axis_index("x")
    for step, term in enumerate(terms):
        rows = pl.ds(pl.multiple_of(((across + step) & 3) * 128, 128), 128)
        for i, (keep, got) in enumerate(((row_keep, row_got), (col_keep, col_got))):
            total = keep[rows, :].astype(F32) + got[rows, :].astype(F32)
            term[:, i * 512 : (i + 1) * 512] = total.astype(BF)


def spread_kernel(*refs):
    given, keep_ref, send_ref, total = refs[:4], refs[4], refs[5], refs[6]
    total[...] = sum(ref[...].astype(F32) for ref in given).astype(BF)
    high = lax.axis_index("yh")
    keep_ref[...] = total[pl.ds(pl.multiple_of(high * 64, 64), 64), :]
    send_ref[...] = total[pl.ds(pl.multiple_of((high ^ 1) * 64, 64), 64), :]


def line_kernel(keep_ref, got_ref, out_ref):
    total = (keep_ref[...].astype(F32) + got_ref[...].astype(F32)).astype(BF)
    row = lax.broadcasted_iota(jnp.int32, (256, 64), 0)
    col = lax.broadcasted_iota(jnp.int32, (256, 64), 1)
    out = jnp.zeros((256, 256), F32)
    for b in range(4):
        here = (col == member(row >> 3, 2, BEGIN_LAST) * 2 + (row & 1)) & ((row & 6) == 2 * b)
        out += product(here.astype(F32).astype(BF), total[:, b * 256 : (b + 1) * 256])
    out_ref[...] = out.astype(BF)


def last_kernel(line_ref, value_ref, out_ref):
    total = jnp.sum(line_ref[...].astype(F32).reshape(32, 8, 256), axis=0)
    for kind in range(2):
        value_ref[:, kind * 256 : (kind + 1) * 256] = total[kind * 4 : kind * 4 + 2]
        out_ref[:, kind * 256 : (kind + 1) * 256] = total[kind * 4 + 2 : kind * 4 + 4]


def final_kernel(row_ref, col_ref, *refs):
    weights, (mixed_ref, gt_ref, row, w_ref, sems) = refs[:8], refs[8:]
    copies = start_copies(weight_copies(weights, w_ref, sems, 2)[0] + [(row_ref, row)], sems)
    first, second = separate(col_ref[...])
    wait_for(copies)
    sides = (
        (row[:, 0:256], row[:, 256:1024]),
        (first[:, 0:256], jnp.concatenate([first[:, 256:512], second], axis=1)),
    )
    for half in range(2):
        for b in range(2):
            total = jnp.zeros((256, 256), F32)
            for kind in range(2):
                block = w_ref[half, kind * 4 : kind * 4 + 4, b * 64 : (b + 1) * 64, 768:1024]
                total += product(sides[kind][0], block.reshape(256, 256))
            start = half * 512 + b * 256
            mixed_ref[:, start : start + 256] = total.astype(BF)
    total = jnp.zeros(gt_ref.shape, F32)
    for kind in range(2):
        total += product(sides[kind][1], w_ref[kind, :, :, 0:768].reshape(1024, 768), LAST)
    gt_ref[...] = total.astype(BF)


def shape(*dims):
    return jax.ShapeDtypeStruct(dims, BF)


def buffer(*dims):
    return pltpu.VMEM(dims, BF)


def cost(flops, moved):
    return pl.CostEstimate(flops=flops, bytes_accessed=moved, transcendentals=0)


def one_hot(index, size):
    return (index[:, None] == jnp.arange(size)[None, :]).astype(BF)


def biases(row_mask, column_mask):
    position = jnp.arange(256)
    seen = position[:, None] >= position[None, :]
    row_in = one_hot(position // ROWBLK, 2)
    row_blocks = jnp.einsum(
        "ia,hab,jb->hij", row_in, row_mask[:, 0].astype(BF), row_in, preferred_element_type=BF
    )
    same = (position[:, None] % 4) == (position[None, :] % 4)
    col_left = one_hot((position % 4) * 8 + position // (4 * COLBLK), 32)
    col_right = one_hot(position // (4 * COLBLK), 8)
    col_blocks = jnp.einsum(
        "ia,hab,jb->hij",
        col_left,
        column_mask.reshape(4, 32, 8).astype(BF),
        col_right,
        preferred_element_type=BF,
    )
    row_bias = jnp.where((row_blocks > 0.5) & seen, 0.0, MASKED).astype(BF)
    col_bias = jnp.where((col_blocks > 0.5) & seen & same, 0.0, MASKED).astype(BF)
    return row_bias, col_bias


def body(tokens, cotangent, row_mask, column_mask, w_query, w_key, w_value, w_out):
    flat = tokens.reshape(256, 1024)
    cot_flat = cotangent.reshape(256, 1024)
    seq = ("z", "yl", "c")

    sent = pl.pallas_call(
        interleave_kernel,
        out_shape=shape(512, 1024),
        in_specs=[VMEM] * 2,
        out_specs=HBM,
        scratch_shapes=[buffer(512, 1024), pltpu.SemaphoreType.DMA((4,))],
        compiler_params=room(16),
        cost_estimate=cost(540000000, 2000000),
        name="interleave",
    )(flat, cot_flat)
    packed = pl.pallas_call(
        pack_kernel,
        out_shape=shape(128, 1024),
        in_specs=[HBM] * 4,
        out_specs=VMEM,
        scratch_shapes=[pltpu.SemaphoreType.DMA((5,))],
        compiler_params=room(60),
        cost_estimate=cost(1000000000, 2000000),
        name="pack",
    )(w_query, w_key, w_value, w_out)
    with jax.named_scope("to_columns"):
        both = lax.all_to_all(
            sent.reshape(64, 8, 1024), seq, split_axis=0, concat_axis=0, tiled=True, axis_index_groups=groups(4, BEGIN)
        ).reshape(512, 1024)
    with jax.named_scope("masks"):
        row_bias, col_bias = biases(row_mask, column_mask)
    with jax.named_scope("weights"):
        flipped = lax.ppermute(packed, ("yh", "yl"), [(y, 3 - y) for y in range(4)])
        pair = pl.pallas_call(
            pair_kernel,
            out_shape=shape(2, 128, 1024),
            in_specs=[VMEM] * 2,
            out_specs=VMEM,
            compiler_params=room(16),
            cost_estimate=cost(PAIR, 1000000),
            name="pair",
        )(packed, flipped)
        weights = [pair] + [
            lax.ppermute(pair, "x", [(x, (x + step) % 4) for x in range(4)]) for step in (1, 2, 3)
        ]
        weights[3], row_bias, col_bias = lax.optimization_barrier((weights[3], row_bias, col_bias))
        weights += [lax.ppermute(part, "c", SWAP) for part in weights]
    row_parts, row_keep, row_send = pl.pallas_call(
        row_kernel,
        out_shape=(shape(256, 1024), shape(512, 512), shape(512, 512)),
        in_specs=[HBM] * 11,
        out_specs=(VMEM,) * 3,
        scratch_shapes=[
            buffer(256, 1024),
            buffer(256, 1024),
            buffer(4, 256, 256),
            buffer(2, 8, 128, 1024),
            pltpu.SemaphoreType.DMA((27,)),
        ],
        compiler_params=room(58),
        cost_estimate=cost(1400000000, 12000000),
        name="row_heads",
    )(flat, cot_flat, row_bias, *weights)
    row_got = lax.ppermute(row_send, "c", SWAP)
    both, row_keep = lax.optimization_barrier((both, row_keep))
    col_parts, col_keep, col_send = pl.pallas_call(
        column_kernel,
        out_shape=(shape(512, 512),) * 3,
        in_specs=[HBM] * 10,
        out_specs=(HBM,) * 3,
        scratch_shapes=[
            buffer(512, 512),
            buffer(512, 512),
            buffer(512, 512),
            buffer(512, 1024),
            buffer(256, 1024),
            buffer(256, 1024),
            buffer(4, 256, 256),
            buffer(2, 8, 128, 1024),
            pltpu.SemaphoreType.DMA((26,)),
        ],
        compiler_params=room(58),
        cost_estimate=cost(1900000000, 8000000),
        name="column_heads",
    )(both, col_bias, *weights)
    col_got = lax.ppermute(col_send, "c", SWAP)
    with jax.named_scope("from_columns"):
        returned = lax.all_to_all(
            col_parts.reshape(64, 8, 512), seq, split_axis=0, concat_axis=0, tiled=True, axis_index_groups=groups(4, BEGIN)
        ).reshape(512, 512)

    with jax.named_scope("gradient_sums"):
        terms = pl.pallas_call(
            pick_kernel,
            out_shape=(shape(128, 1024),) * 4,
            in_specs=[VMEM] * 4,
            out_specs=(VMEM,) * 4,
            compiler_params=room(16),
            cost_estimate=cost(PICK, 3000000),
            name="pick",
        )(row_keep, row_got, col_keep, col_got)
        moved = [
            lax.ppermute(terms[step], "x", [(x, (x + step) % 4) for x in range(4)])
            for step in (2, 1, 3)
        ]
        line_keep, line_send = pl.pallas_call(
            spread_kernel,
            out_shape=(shape(64, 1024),) * 2,
            in_specs=[VMEM] * 4,
            out_specs=(VMEM,) * 2,
            scratch_shapes=[buffer(128, 1024)],
            compiler_params=room(16),
            cost_estimate=cost(10000000, 1000000),
            name="spread",
        )(terms[0], *moved)
        line_got = lax.ppermute(line_send, ("yh", "yl"), [(y, 3 - y) for y in range(4)])
        line = pl.pallas_call(
            line_kernel,
            out_shape=shape(256, 256),
            in_specs=[VMEM] * 2,
            out_specs=VMEM,
            compiler_params=room(16),
            cost_estimate=cost(10000000, 300000),
            name="line",
        )(line_keep, line_got)
        line, returned = lax.optimization_barrier((line, returned))
        line = lax.all_to_all(
            line.reshape(32, 8, 256), ("z", "yl"), split_axis=0, concat_axis=0, tiled=True, axis_index_groups=groups(2, BEGIN_LAST)
        )
        grad_value, grad_output = pl.pallas_call(
            last_kernel,
            out_shape=(jax.ShapeDtypeStruct((2, 512), F32),) * 2,
            in_specs=[VMEM],
            out_specs=(VMEM,) * 2,
            compiler_params=room(16),
            cost_estimate=cost(100000, 100000),
            name="last",
        )(line.reshape(256, 256))
        grad_output = jnp.transpose(grad_output)
    mixed, grad_tokens = pl.pallas_call(
        final_kernel,
        out_shape=(shape(256, 1024), shape(256, 1024)),
        in_specs=[HBM, VMEM] + [HBM] * 8,
        out_specs=(VMEM, VMEM),
        scratch_shapes=[
            buffer(256, 1024),
            buffer(2, 8, 128, 1024),
            pltpu.SemaphoreType.DMA((17,)),
        ],
        compiler_params=room(58),
        cost_estimate=cost(1200000000, 8000000),
        name="output_products",
    )(row_parts, returned, *weights)
    return (
        mixed.reshape(tokens.shape),
        grad_tokens.reshape(tokens.shape),
        grad_value,
        grad_output,
    )


def solution(mesh):
    fine = Mesh(mesh.devices.reshape(4, 2, 16, 2, 2), ("x", "yh", "z", "yl", "c"))
    dp, seq = ("x", "yh"), ("z", "yl", "c")
    return jax.shard_map(
        body,
        mesh=fine,
        in_specs=(
            P(dp, seq, None, None),
            P(dp, seq, None, None),
            P(None, seq, None, None),
            P(None, seq, None, None),
            P(dp, None),
            P(dp, None),
            P(dp, None),
            P(dp, None),
        ),
        out_specs=(
            P(dp, seq, None, None),
            P(dp, seq, None, None),
            P(dp + seq, None),
            P(None, dp + seq),
        ),
        check_vma=False,
    )
```
